32 devices in a mesh: group: 2 (over x), pts: 16 (over z, y, core).
Axes of the slice: x: 2, y: 2, z: 4, core: 2. Of those that a mesh axis runs over, the one named last changes fastest.
Arguments:
- coords: int32 [3, 49152], P(None, ('group', 'pts')), parts along dimension 1, may hold values from 0 to 1023
- field: bfloat16 [64, 49152], P(None, ('group', 'pts')), parts along dimension 1, may hold values from -6 to 6
- mode_list: int32 [4096], replicated, may hold values from 0 to 4095, each once
- spec_weight: bfloat16 [2, 4096, 2, 64, 64], P(None, 'pts'), may hold values from -0.5 to 0.5
- bypass_weight: bfloat16 [2, 64, 64], replicated, may hold values from -0.75 to 0.75
- bypass_bias: float32 [2, 64], replicated, may hold values from -3 to 3
Outputs:
- output: bfloat16 [64, 49152], P(None, ('group', 'pts')), parts along dimension 1
The draws below stay inside these ranges and needn't reach their ends.
There are 2 independent parts, one for each index of `group`. The reference program is written for one: setup_inputs(seed, part) draws one part's arguments, and reference() takes and returns one part's arrays. A program takes and returns all parts, laid end to end along the dimension named above; an argument that names none is the same for every part. Nothing has to cross between parts.
Inputs may be any that keep to these rules, and one draw needn't show every extreme that they name: `mode_list`: each of the 4096 mode numbers appears exactly once.
All inputs are finite; a program needn't handle non-finite values.
Results may differ from the reference program's by a relative error of at most 0.0059.
Values may be sent and summed in bfloat16 or wider, within the bound.
No kernel may reach another device: no remote copies, remote signals or barrier semaphores. Data moves between devices by JAX's collectives and lax.ppermute only.
A program may use at most 192 MiB of HBM per device.

```python
import math
import jax
import jax.numpy as jnp
from jax import lax

C = 64
KDIM = 16
GRID = 1024
LAYERS = 2
MODES = 4096
POINTS = 24576


def set_ends(array, stream_key, least, largest):
    dims = array.shape
    index_at = [jax.random.randint(jax.random.fold_in(stream_key, axis), (), 0, dims[axis]) for axis in range(len(dims))]
    array = array.at[tuple(index_at)].set(least)
    longest = dims.index(max(dims))
    index_at[longest] = (index_at[longest] + 1) % dims[longest]
    return array.at[tuple(index_at)].set(largest)


def shard_levels(stream_key, shape, pieces, low, top_value):
    gain = 1.0
    for dim, shards_of in pieces:
        draws = jax.random.uniform(jax.random.fold_in(jax.random.fold_in(stream_key, 6), dim), (shards_of,), jnp.float32, low / len(pieces), top_value / len(pieces))
        gain = gain * jnp.repeat(jnp.exp(draws), shape[dim] // shards_of).reshape((-1,) + (1,) * (len(shape) - 1 - dim))
    return gain


def noise(own_key, shape, deviation, reach, cuts=(), dtype=jnp.bfloat16):
    result = deviation * jax.random.normal(own_key, shape, jnp.float32)
    if cuts:
        result = result * shard_levels(own_key, shape, cuts, -0.22, 0.18)
    return jnp.clip(result, -reach, reach).astype(dtype)


def setup_inputs(seed: int = 0, part: int = 0) -> dict:
    key_list = jax.random.split(jax.random.key(seed), 7)
    part_splits = jax.random.split(jax.random.fold_in(key_list[6], part), 7)
    return {
        "coords": set_ends(jax.random.randint(part_splits[0], (3, POINTS), 0, GRID), jax.random.fold_in(part_splits[0], 1), 0, GRID - 1).astype(jnp.int32),
        "field": noise(part_splits[1], (C, POINTS), 1.0, 6.0, ((1, 16),)),
        "mode_list": jax.random.permutation(key_list[2], MODES).astype(jnp.int32),
        "spec_weight": noise(key_list[3], (LAYERS, MODES, 2, C, C), (2 * C) ** -0.5, 0.5, ((1, 16),)),
        "bypass_weight": noise(key_list[4], (LAYERS, C, C), C ** -0.5, 0.75),
        "bypass_bias": noise(key_list[5], (LAYERS, C), 0.5, 3.0, (), jnp.float32),
    }


TWO_PI = 2.0 * math.pi

def direct_basis(wave_ids, coords):
    centre = KDIM // 2
    wave_x = wave_ids // (KDIM * KDIM) - centre
    wave_y = wave_ids // KDIM % KDIM - centre
    wave_z = wave_ids % KDIM - centre
    phase_index = wave_x[:, None] * coords[0][None, :] + wave_y[:, None] * coords[1][None, :] + wave_z[:, None] * coords[2][None, :]
    phase_index = jnp.mod(phase_index, GRID)
    radians = phase_index.astype(jnp.float32) * (TWO_PI / GRID)
    return jnp.concatenate([jnp.cos(radians).astype(jnp.bfloat16), (-jnp.sin(radians)).astype(jnp.bfloat16)], 0)

def mix_modes(spectrum, weights):
    width = weights.shape[-1]
    real_in = spectrum[:, :width]
    imag_in = spectrum[:, width:]
    weight_real = weights[:, 0].astype(jnp.float32)
    weight_imag = weights[:, 1].astype(jnp.float32)
    high = lax.Precision.HIGHEST
    real_out = jnp.einsum('kc,kcd->kd', real_in, weight_real, precision=high) - jnp.einsum('kc,kcd->kd', imag_in, weight_imag, precision=high)
    imag_out = jnp.einsum('kc,kcd->kd', real_in, weight_imag, precision=high) + jnp.einsum('kc,kcd->kd', imag_in, weight_real, precision=high)
    return jnp.concatenate([real_out, imag_out], 1).astype(jnp.bfloat16)

def finish_layer(spectral, field, layer_weight, layer_bias, modes_total):
    direct = lax.dot_general(layer_weight, field, (((0,), (0,)), ((), ())), preferred_element_type=jnp.float32)
    summed = spectral * (1.0 / math.sqrt(modes_total)) + direct + layer_bias[:, None]
    return jax.nn.gelu(summed, approximate=False).astype(jnp.bfloat16)

def reference(coords, field, mode_list, spec_weight, bypass_weight, bypass_bias):
    block_size = math.gcd(MODES, 256)
    block_count = MODES // block_size
    wave_blocks = mode_list.reshape(block_count, block_size)
    normaliser = 1.0 / math.sqrt(POINTS)
    for depth in range(LAYERS):
        current = field

        def forward_block(wave_ids):
            basis = direct_basis(wave_ids, coords)
            product = lax.dot_general(basis, current, (((1,), (1,)), ((), ())), preferred_element_type=jnp.float32) * normaliser
            return jnp.concatenate([product[:block_size], product[block_size:]], 1)
        spectrum = lax.map(forward_block, wave_blocks).reshape(MODES, 2 * C)
        mixed = mix_modes(spectrum, spec_weight[depth])

        def inverse_block(running, inputs):
            wave_ids, coeffs = inputs
            basis = direct_basis(wave_ids, coords)
            stacked = jnp.concatenate([coeffs[:, :C], coeffs[:, C:]], 0)
            return (running + lax.dot_general(stacked, basis, (((0,), (0,)), ((), ())), preferred_element_type=jnp.float32), None)
        start_value = jnp.zeros((C, POINTS), jnp.float32)
        spectral, unused = lax.scan(inverse_block, start_value, (wave_blocks, mixed.reshape(block_count, block_size, 2 * C)))
        field = finish_layer(spectral, current, bypass_weight[depth], bypass_bias[depth], MODES)
    return field
```

```python
import math

import jax
import jax.numpy as jnp
import numpy as np
from jax import lax
from jax.experimental import pallas as pl
from jax.experimental.pallas import tpu as pltpu
from jax.sharding import PartitionSpec as P

KDIM = 16
GRID = 1024
LAYERS = 2
TWO_PI = 2.0 * math.pi
HALF = KDIM // 2
KZ = HALF + 1
GROUPS = HALF + 3
ROWS_A = GROUPS * 32
ROWS_Q = KZ * ROWS_A
VMEM = 56 * 1024 * 1024
F32 = jnp.float32
BF16 = jnp.bfloat16


def params():
    return pltpu.CompilerParams(vmem_limit_bytes=VMEM)


def vmem():
    return pl.BlockSpec(memory_space=pltpu.VMEM)


def smem():
    return pl.BlockSpec(memory_space=pltpu.SMEM)


def table_rows(mode_list):
    kx = mode_list // (KDIM * KDIM) - HALF
    ky = mode_list // KDIM % KDIM - HALF
    kz = mode_list % KDIM - HALF
    flip = kx < 0
    ky = jnp.where(flip, -ky, ky)
    kz = jnp.where(flip, -kz, kz)
    ax, ay, az = jnp.abs(kx), jnp.abs(ky), jnp.abs(kz)
    quarter = 2 * (ky < 0).astype(jnp.int32) + (kz < 0).astype(jnp.int32)
    group = jnp.where(ay < HALF, ax, jnp.where(ax < HALF, HALF + 1, HALF + 2))
    inner = jnp.where(ay < HALF, ay, jnp.where(ax < HALF, ax, 0))
    row = ((az * GROUPS + group) * 4 + quarter) * 8 + inner
    return row, flip


def tables_kernel(coords_ref, a_ref, cs_ref):
    angle = coords_ref[...].astype(F32) * (TWO_PI / GRID)
    one_c, one_s = jnp.cos(angle), jnp.sin(angle)
    cos, sin = [jnp.ones_like(angle), one_c], [jnp.zeros_like(angle), one_s]
    for k in range(2, HALF + 1):
        i, j = k // 2, k - k // 2
        cos.append(cos[i] * cos[j] - sin[i] * sin[j])
        sin.append(sin[i] * cos[j] + cos[i] * sin[j])
    cx = jnp.concatenate([c[0:1] for c in cos[:HALF]], 0)
    sx = jnp.concatenate([s[0:1] for s in sin[:HALF]], 0)
    cy = jnp.concatenate([c[1:2] for c in cos[:HALF]], 0)
    sy = jnp.concatenate([s[1:2] for s in sin[:HALF]], 0)
    for g in range(GROUPS):
        if g <= HALF:
            c, s = cos[g][0:1], sin[g][0:1]
            parts = [c * cy, c * sy, s * cy, s * sy]
        elif g == HALF + 1:
            c, s = cos[HALF][1:2], sin[HALF][1:2]
            parts = [cx * c, cx * s, sx * c, sx * s]
        else:
            c, s = cos[HALF][1:2], sin[HALF][1:2]
            first = (lax.broadcasted_iota(jnp.int32, cx.shape, 0) == 0).astype(F32)
            cl, sl = first * cos[HALF][0:1], first * sin[HALF][0:1]
            parts = [cl * c, cl * s, sl * c, sl * s]
        a_ref[g * 32 : (g + 1) * 32, :] = jnp.concatenate(parts, 0).astype(BF16)
    pad = jnp.zeros((7, angle.shape[1]), F32)
    cs_ref[...] = jnp.concatenate(
        [c[2:3] for c in cos] + [pad] + [s[2:3] for s in sin] + [pad], 0
    )


def make_tables(coords):
    points = coords.shape[1]
    return pl.pallas_call(
        tables_kernel,
        out_shape=(
            jax.ShapeDtypeStruct((ROWS_A, points), BF16),
            jax.ShapeDtypeStruct((32, points), F32),
        ),
        in_specs=[vmem()],
        out_specs=(vmem(), vmem()),
        compiler_params=params(),
    )(coords)


def sign_lanes(width):
    lane = lax.broadcasted_iota(jnp.int32, (8, 2 * width), 1)
    return jnp.where(lane < width, 1.0, -1.0).astype(F32)


def forward_kernel(norm, a_ref, cs_ref, own_ref, other_ref, q_ref, hs_ref, b_ref):
    width = own_ref.shape[0]
    points = own_ref.shape[1]
    hs_ref[:, :points] = own_ref[...].astype(F32) * norm
    hs_ref[:, points:] = other_ref[...].astype(F32) * norm

    def product(b):
        return lax.dot_general(
            a_ref[...], b, (((1,), (1,)), ((), ())), preferred_element_type=F32
        )

    first = product(hs_ref[...].astype(BF16))
    q_ref[0:ROWS_A, :] = jnp.concatenate([first, jnp.zeros_like(first)], 1)

    for pair in range(HALF // 2):
        for half in range(2):
            k = 2 * pair + 1 + half
            b_ref[2 * half * width : (2 * half + 1) * width, :] = (
                hs_ref[...] * cs_ref[k : k + 1, :]
            ).astype(BF16)
            b_ref[(2 * half + 1) * width : (2 * half + 2) * width, :] = (
                hs_ref[...] * cs_ref[16 + k : 17 + k, :]
            ).astype(BF16)
        both = product(b_ref[...])
        k = 2 * pair + 1
        q_ref[k * ROWS_A : (k + 1) * ROWS_A, :] = both[:, : 2 * width]
        q_ref[(k + 1) * ROWS_A : (k + 2) * ROWS_A, :] = both[:, 2 * width :]

    sign = sign_lanes(width)

    def combine(i, carry):
        base = pl.multiple_of(i * 32, 32)
        cc = q_ref[pl.ds(base, 8), :]
        cs = q_ref[pl.ds(base + 8, 8), :]
        sc = q_ref[pl.ds(base + 16, 8), :]
        ss = q_ref[pl.ds(base + 24, 8), :]
        for y in range(2):
            u = cc + ss if y else cc - ss
            v = pltpu.roll(sc - cs if y else sc + cs, width, 1)
            q_ref[pl.ds(base + 16 * y, 8), :] = u * sign - v
            q_ref[pl.ds(base + 16 * y + 8, 8), :] = u + v * sign
        return carry

    lax.fori_loop(0, KZ * GROUPS, combine, 0, unroll=3)


def gather_rows(idx_ref, q_ref, out_ref, offset):
    def step(j, carry):
        out_ref[pl.ds(j, 1), :] = q_ref[pl.ds(idx_ref[offset + j], 1), :]
        return carry

    lax.fori_loop(0, out_ref.shape[0], step, 0, unroll=16)


def forward(idx, a, cs, own, other, norm, rows):
    width, points = own.shape
    kept = rows // 2

    def kernel(idx_ref, a_ref, cs_ref, own_ref, other_ref, keep_ref, send_ref, q_ref, hs_ref, b_ref, stage_ref):
        forward_kernel(norm, a_ref, cs_ref, own_ref, other_ref, q_ref, hs_ref, b_ref)
        gather_rows(idx_ref, q_ref, stage_ref, kept)
        send_ref[...] = stage_ref[...].astype(BF16)
        gather_rows(idx_ref, q_ref, keep_ref, 0)

    return pl.pallas_call(
        kernel,
        out_shape=(
            jax.ShapeDtypeStruct((kept, 2 * width), F32),
            jax.ShapeDtypeStruct((kept, 2 * width), BF16),
        ),
        in_specs=[smem()] + [vmem()] * 4,
        out_specs=(vmem(), vmem()),
        scratch_shapes=[
            pltpu.VMEM((ROWS_Q, 2 * width), F32),
            pltpu.VMEM((width, 2 * points), F32),
            pltpu.VMEM((4 * width, 2 * points), BF16),
            pltpu.VMEM((kept, 2 * width), F32),
        ],
        compiler_params=params(),
    )(idx, a, cs, own, other)


def mix_kernel(scale, keep_ref, got_ref, flip_ref, w_ref, out_ref, s_ref, acc_ref):
    step = pl.program_id(0)
    width = acc_ref.shape[0] // 2

    @pl.when(step == 0)
    def _():
        total = keep_ref[...] + got_ref[...].astype(F32)
        s_ref[...] = total.T
        s_ref[width:, :] = s_ref[width:, :] * flip_ref[...]
        acc_ref[...] = jnp.zeros_like(acc_ref)

    block = w_ref.shape[2]
    real, imag = acc_ref[:width, :], acc_ref[width:, :]
    for i in range(block):
        row = step * block + i
        re = s_ref[pl.ds(row, 1), :]
        im = s_ref[pl.ds(width + row, 1), :]
        wr = w_ref[0, 0, i].astype(F32)
        wi = w_ref[0, 1, i].astype(F32)
        real = real + re * wr - im * wi
        imag = imag + re * wi + im * wr
    acc_ref[:width, :] = real
    acc_ref[width:, :] = imag

    @pl.when(step == pl.num_programs(0) - 1)
    def _():
        acc_ref[:width, :] = acc_ref[:width, :] * scale
        acc_ref[width:, :] = acc_ref[width:, :] * (flip_ref[...] * scale)
        out_ref[...] = acc_ref[...].T.astype(BF16)


def mix(keep, got, flip, weights, layer, scale):
    modes, double = keep.shape
    width = double // 2
    block = 8

    def kernel(*refs):
        mix_kernel(scale, *refs)

    fixed = lambda i: (0, 0)
    return pl.pallas_call(
        kernel,
        grid=(width // block,),
        out_shape=jax.ShapeDtypeStruct((modes, double), BF16),
        in_specs=[
            pl.BlockSpec((modes, double), fixed),
            pl.BlockSpec((modes, double), fixed),
            pl.BlockSpec((1, modes), fixed),
            pl.BlockSpec((1, 2, block, width, modes), lambda i: (layer, 0, i, 0, 0)),
        ],
        out_specs=pl.BlockSpec((modes, double), fixed),
        scratch_shapes=[pltpu.VMEM((double, modes), F32), pltpu.VMEM((double, modes), F32)],
        compiler_params=params(),
    )(keep, got, flip, weights)


def inverse_kernel(idx_ref, a_ref, cs_ref, mixed_ref, own_ref, other_ref, z_ref, m_ref, t_ref):
    width = own_ref.shape[0]
    points = own_ref.shape[1]
    m_ref[...] = mixed_ref[...].astype(F32)

    def clear(i, carry):
        z_ref[pl.ds(pl.multiple_of(i * 32, 32), 32), :] = jnp.zeros((32, 2 * width), F32)
        return carry

    lax.fori_loop(0, 2 * ROWS_Q // 32, clear, 0, unroll=6)

    def place(j, carry):
        z_ref[pl.ds(idx_ref[j], 1), :] = m_ref[pl.ds(j, 1), :]
        return carry

    lax.fori_loop(0, m_ref.shape[0], place, 0, unroll=16)
    sign = sign_lanes(width)

    def combine(i, carry):
        base = pl.multiple_of(i * 32, 32)
        u, v = [], []
        for y in range(2):
            lo = base + 16 * y
            plus = z_ref[pl.ds(lo, 8), :] + z_ref[pl.ds(ROWS_Q + lo, 8), :]
            minus = z_ref[pl.ds(lo + 8, 8), :] + z_ref[pl.ds(ROWS_Q + lo + 8, 8), :]
            u.append(plus * sign + minus)
            v.append(pltpu.roll(plus - minus * sign, width, 1))
        z_ref[pl.ds(base, 8), :] = u[0] + u[1]
        z_ref[pl.ds(base + 8, 8), :] = v[1] - v[0]
        z_ref[pl.ds(base + 16, 8), :] = -v[0] - v[1]
        z_ref[pl.ds(base + 24, 8), :] = u[1] - u[0]
        return carry

    lax.fori_loop(0, KZ * GROUPS, combine, 0, unroll=3)
    for k in range(KZ):
        t_ref[k * 2 * width : (k + 1) * 2 * width, :] = z_ref[
            k * ROWS_A : (k + 1) * ROWS_A, :
        ].T.astype(BF16)

    chunk = math.gcd(points, 512)
    for part, out_ref in enumerate((own_ref, other_ref)):
        for at in range(0, points, chunk):
            here = slice(part * points + at, part * points + at + chunk)
            r = lax.dot_general(
                t_ref[...], a_ref[:, here], (((1,), (0,)), ((), ())), preferred_element_type=F32
            )
            total = r[:width]
            for k in range(1, KZ):
                lo = 2 * k * width
                total = total + r[lo : lo + width] * cs_ref[k : k + 1, here]
                total = total + r[lo + width : lo + 2 * width] * cs_ref[16 + k : 17 + k, here]
            out_ref[:, at : at + chunk] = total.astype(out_ref.dtype)


def inverse(idx, a, cs, mixed, points):
    rows, double = mixed.shape
    width = double // 2
    return pl.pallas_call(
        inverse_kernel,
        out_shape=(
            jax.ShapeDtypeStruct((width, points), F32),
            jax.ShapeDtypeStruct((width, points), F32),
        ),
        in_specs=[smem()] + [vmem()] * 3,
        out_specs=(vmem(), vmem()),
        scratch_shapes=[
            pltpu.VMEM((2 * ROWS_Q, double), F32),
            pltpu.VMEM((rows, double), F32),
            pltpu.VMEM((KZ * double, ROWS_A), BF16),
        ],
        compiler_params=params(),
    )(idx, a, cs, mixed)


def body(coords, field, mode_list, spec_weight, bypass_weight, bypass_bias):
    width, points = field.shape
    modes_total = mode_list.shape[0]
    count = lax.axis_size("pts")
    bits = count.bit_length() - 1
    me = lax.axis_index("pts")
    local = modes_total // count
    norm = 1.0 / math.sqrt(points * count)
    scale = 1.0 / math.sqrt(modes_total)

    def swap(x, bit):
        return lax.ppermute(x, "pts", [(i, i ^ (1 << bit)) for i in range(count)])

    row, flip = table_rows(mode_list)
    signs = jnp.where(flip, -1.0, 1.0).astype(F32)
    my_signs = lax.dynamic_slice(signs, (me * local,), (local,)).reshape(1, local)
    place = row + jnp.where(flip, ROWS_Q, 0)
    order = np.array(
        [sum(((t >> (bits - 2 - b)) & 1) << (b + 1) for b in range(bits - 1)) for t in range(count // 2)]
    )
    owners = jnp.bitwise_xor(me, jnp.asarray(order, jnp.int32))
    idx_get = row.reshape(count, local)[owners].reshape(-1)
    idx_put = place.reshape(count, local)[owners].reshape(-1)
    weights = jnp.transpose(spec_weight, (0, 2, 3, 4, 1))

    a, cs = make_tables(jnp.concatenate([coords, swap(coords, 0)], 1))
    for depth in range(LAYERS):
        other = swap(field, 0)
        keep, send = forward(idx_get, a, cs, field, other, norm, modes_total // 2)
        for bit in range(1, bits):
            got = swap(send, bit)
            if bit == bits - 1:
                break
            half = keep.shape[0] // 2
            send = (keep[half:] + got[half:].astype(F32)).astype(BF16)
            keep = keep[:half] + got[:half].astype(F32)
        mixed = mix(keep, got, my_signs, weights, depth, scale)
        for bit in range(bits - 1, 0, -1):
            mixed = jnp.concatenate([mixed, swap(mixed, bit)], 0)
        spectral, theirs = inverse(idx_put, a, cs, mixed, points)
        spectral = spectral + swap(theirs, 0)
        direct = lax.dot_general(
            bypass_weight[depth], field, (((0,), (0,)), ((), ())), preferred_element_type=F32
        )
        summed = spectral + direct + bypass_bias[depth][:, None]
        field = jax.nn.gelu(summed, approximate=False).astype(BF16)
    return field


def solution(mesh):
    placed = (
        P(None, ("group", "pts")),
        P(None, ("group", "pts")),
        P(),
        P(None, "pts", None, None, None),
        P(),
        P(),
    )
    return jax.shard_map(
        body, mesh=mesh, in_specs=placed, out_specs=P(None, ("group", "pts")), check_vma=False
    )
```

```python
import math

import jax
import jax.numpy as jnp
from jax import lax
from jax.experimental import pallas as pl
from jax.experimental.pallas import tpu as pltpu
from jax.sharding import PartitionSpec as P

KDIM = 16
GRID = 1024
LAYERS = 2
TWO_PI = 2.0 * math.pi
HALF = KDIM // 2
KZ = HALF + 1
GROUPS = HALF + 3
ROWS_A = GROUPS * 32
ROWS_Q = KZ * ROWS_A
VMEM = 24 * 1024 * 1024
F32 = jnp.float32
BF16 = jnp.bfloat16


def params():
    return pltpu.CompilerParams(vmem_limit_bytes=VMEM)


def vmem():
    return pl.BlockSpec(memory_space=pltpu.VMEM)


def smem():
    return pl.BlockSpec(memory_space=pltpu.SMEM)


def table_rows(mode_list):
    kx = mode_list // (KDIM * KDIM) - HALF
    ky = mode_list // KDIM % KDIM - HALF
    kz = mode_list % KDIM - HALF
    flip = kx < 0
    ky = jnp.where(flip, -ky, ky)
    kz = jnp.where(flip, -kz, kz)
    ax, ay, az = jnp.abs(kx), jnp.abs(ky), jnp.abs(kz)
    quarter = 2 * (ky < 0).astype(jnp.int32) + (kz < 0).astype(jnp.int32)
    group = jnp.where(ay < HALF, ax, jnp.where(ax < HALF, HALF + 1, HALF + 2))
    inner = jnp.where(ay < HALF, ay, jnp.where(ax < HALF, ax, 0))
    row = ((az * GROUPS + group) * 4 + quarter) * 8 + inner
    return row, flip


def tables_kernel(own_ref, other_ref, a_ref, cs_ref):
    points = jnp.concatenate([own_ref[...], other_ref[...]], 1)
    angle = points.astype(F32) * (TWO_PI / GRID)
    one_c, one_s = jnp.cos(angle), jnp.sin(angle)
    cos, sin = [jnp.ones_like(angle), one_c], [jnp.zeros_like(angle), one_s]
    for k in range(2, HALF + 1):
        i, j = k // 2, k - k // 2
        cos.append(cos[i] * cos[j] - sin[i] * sin[j])
        sin.append(sin[i] * cos[j] + cos[i] * sin[j])
    cx = jnp.concatenate([c[0:1] for c in cos[:HALF]], 0)
    sx = jnp.concatenate([s[0:1] for s in sin[:HALF]], 0)
    cy = jnp.concatenate([c[1:2] for c in cos[:HALF]], 0)
    sy = jnp.concatenate([s[1:2] for s in sin[:HALF]], 0)
    for g in range(GROUPS):
        if g <= HALF:
            c, s = cos[g][0:1], sin[g][0:1]
            parts = [c * cy, c * sy, s * cy, s * sy]
        elif g == HALF + 1:
            c, s = cos[HALF][1:2], sin[HALF][1:2]
            parts = [cx * c, cx * s, sx * c, sx * s]
        else:
            c, s = cos[HALF][1:2], sin[HALF][1:2]
            first = (lax.broadcasted_iota(jnp.int32, cx.shape, 0) == 0).astype(F32)
            cl, sl = first * cos[HALF][0:1], first * sin[HALF][0:1]
            parts = [cl * c, cl * s, sl * c, sl * s]
        a_ref[g * 32 : (g + 1) * 32, :] = jnp.concatenate(parts, 0).astype(BF16)
    pad = jnp.zeros((7, angle.shape[1]), F32)
    cs_ref[...] = jnp.concatenate(
        [c[2:3] for c in cos] + [pad] + [s[2:3] for s in sin] + [pad], 0
    )


def make_tables(own, other):
    points = 2 * own.shape[1]
    return pl.pallas_call(
        tables_kernel,
        out_shape=(
            jax.ShapeDtypeStruct((ROWS_A, points), BF16),
            jax.ShapeDtypeStruct((32, points), F32),
        ),
        in_specs=[vmem(), vmem()],
        out_specs=(vmem(), vmem()),
        compiler_params=params(),
    )(own, other)


def sign_lanes(width):
    lane = lax.broadcasted_iota(jnp.int32, (8, 2 * width), 1)
    return jnp.where(lane < width, 1.0, -1.0).astype(F32)


def owners_of(count):
    bits = count.bit_length() - 1
    return [
        sum(((t >> (bits - 2 - b)) & 1) << (b + 1) for b in range(bits - 1))
        for t in range(count // 2)
    ]


def spectrum(norm, a_ref, cs_ref, own_ref, other_ref, q_ref, hs_ref, b_refs):
    width, points = own_ref.shape
    hs_ref[:, :points] = own_ref[...].astype(F32) * norm
    hs_ref[:, points:] = other_ref[...].astype(F32) * norm

    def product(b):
        return lax.dot_general(
            a_ref[...], b, (((1,), (1,)), ((), ())), preferred_element_type=F32
        )

    first = product(hs_ref[...].astype(BF16))
    q_ref[0:ROWS_A, :] = jnp.concatenate([first, jnp.zeros_like(first)], 1)

    for pair in range(HALF // 2):
        b_ref = b_refs[pair % 2]
        for half in range(2):
            k = 2 * pair + 1 + half
            b_ref[2 * half * width : (2 * half + 1) * width, :] = (
                hs_ref[...] * cs_ref[k : k + 1, :]
            ).astype(BF16)
            b_ref[(2 * half + 1) * width : (2 * half + 2) * width, :] = (
                hs_ref[...] * cs_ref[16 + k : 17 + k, :]
            ).astype(BF16)
        both = product(b_ref[...])
        k = 2 * pair + 1
        q_ref[k * ROWS_A : (k + 1) * ROWS_A, :] = both[:, : 2 * width]
        q_ref[(k + 1) * ROWS_A : (k + 2) * ROWS_A, :] = both[:, 2 * width :]

    sign = sign_lanes(width)

    def combine(i, carry):
        base = pl.multiple_of(i * 32, 32)
        cc = q_ref[pl.ds(base, 8), :]
        cs = q_ref[pl.ds(base + 8, 8), :]
        sc = q_ref[pl.ds(base + 16, 8), :]
        ss = q_ref[pl.ds(base + 24, 8), :]
        for y in range(2):
            u = cc + ss if y else cc - ss
            v = pltpu.roll(sc - cs if y else sc + cs, width, 1)
            q_ref[pl.ds(base + 16 * y, 8), :] = u * sign - v
            q_ref[pl.ds(base + 16 * y + 8, 8), :] = u + v * sign
        return carry

    lax.fori_loop(0, KZ * GROUPS, combine, 0, unroll=9)


def gather_rows(row_ref, me_ref, q_ref, out_ref, owners, local):
    for at, owner in enumerate(owners):
        base = jnp.bitwise_xor(me_ref[0], owner) * local

        def step(j, carry, base=base, at=at):
            out_ref[pl.ds(at * local + j, 1), :] = q_ref[pl.ds(row_ref[base + j], 1), :]
            return carry

        lax.fori_loop(0, local, step, 0, unroll=32)


def forward(rows, me, a, cs, own, other, norm, owners, local):
    width, points = own.shape
    sent = len(owners) * local

    def kernel(row_ref, me_ref, a_ref, cs_ref, own_ref, other_ref, q_ref, send_ref, hs_ref, b0_ref, b1_ref, stage_ref):
        spectrum(norm, a_ref, cs_ref, own_ref, other_ref, q_ref, hs_ref, (b0_ref, b1_ref))
        gather_rows(row_ref, me_ref, q_ref, stage_ref, owners, local)
        send_ref[...] = stage_ref[...].astype(BF16)

    return pl.pallas_call(
        kernel,
        out_shape=(
            jax.ShapeDtypeStruct((ROWS_Q, 2 * width), F32),
            jax.ShapeDtypeStruct((sent, 2 * width), BF16),
        ),
        in_specs=[smem()] * 2 + [vmem()] * 4,
        out_specs=(vmem(), vmem()),
        scratch_shapes=[
            pltpu.VMEM((width, 2 * points), F32),
            pltpu.VMEM((4 * width, 2 * points), BF16),
            pltpu.VMEM((4 * width, 2 * points), BF16),
            pltpu.VMEM((sent, 2 * width), F32),
        ],
        compiler_params=params(),
        name="forward",
    )(rows, me, a, cs, own, other)


def keep_rows(rows, me, q, owners, local):
    def kernel(row_ref, me_ref, q_ref, out_ref):
        gather_rows(row_ref, me_ref, q_ref, out_ref, owners, local)

    return pl.pallas_call(
        kernel,
        out_shape=jax.ShapeDtypeStruct((len(owners) * local, q.shape[1]), F32),
        in_specs=[smem()] * 2 + [vmem()],
        out_specs=vmem(),
        compiler_params=params(),
        name="keep_rows",
    )(rows, me, q)


def mix(keep, got, flip, weights, layer, scale):
    modes, double = keep.shape
    width = double // 2
    block = 16

    def kernel(keep_ref, got_ref, flip_ref, w_ref, out_ref, s_ref, acc_ref):
        step = pl.program_id(0)

        @pl.when(step == 0)
        def _():
            s_ref[...] = (keep_ref[...] + got_ref[...].astype(F32)).T
            s_ref[width:, :] = s_ref[width:, :] * flip_ref[...]

        def add(i, carry):
            real, imag = carry
            re = s_ref[pl.ds(i, 1), :]
            im = s_ref[pl.ds(width + i, 1), :]
            wr = w_ref[0, 0, i].astype(F32)
            wi = w_ref[0, 1, i].astype(F32)
            return real + re * wr - im * wi, imag + re * wi + im * wr

        zero = jnp.zeros((block, modes), F32)
        real, imag = lax.fori_loop(0, width, add, (zero, zero), unroll=16)
        at = pl.multiple_of(step * block, block)
        acc_ref[pl.ds(at, block), :] = real * scale
        acc_ref[pl.ds(width + at, block), :] = imag * (flip_ref[...] * scale)

        @pl.when(step == pl.num_programs(0) - 1)
        def _():
            out_ref[...] = acc_ref[...].T.astype(BF16)

    fixed = lambda i: (0, 0)
    return pl.pallas_call(
        kernel,
        grid=(width // block,),
        out_shape=jax.ShapeDtypeStruct((modes, double), BF16),
        in_specs=[
            pl.BlockSpec((modes, double), fixed),
            pl.BlockSpec((modes, double), fixed),
            pl.BlockSpec((1, modes), fixed),
            pl.BlockSpec((1, 2, width, block, modes), lambda i: (layer, 0, 0, i, 0)),
        ],
        out_specs=pl.BlockSpec((modes, double), fixed),
        scratch_shapes=[pltpu.VMEM((double, modes), F32), pltpu.VMEM((double, modes), F32)],
        compiler_params=params(),
        name="mix",
    )(keep, got, flip, weights)


def place_rows(place_ref, me_ref, m_ref, z_ref, owners, local):
    for at, owner in enumerate(owners):
        base = jnp.bitwise_xor(me_ref[0], owner) * local

        def step(j, carry, base=base, at=at):
            z_ref[pl.ds(place_ref[base + j], 1), :] = m_ref[pl.ds(at * local + j, 1), :]
            return carry

        lax.fori_loop(0, local, step, 0, unroll=32)


def place_first(places, me, pieces, owners, local):
    double = pieces[0].shape[1]
    count = len(owners) * local
    n = len(pieces)

    def kernel(place_ref, me_ref, *refs):
        z_ref, m_ref = refs[n:]
        at = 0
        for ref in refs[:n]:
            m_ref[at : at + ref.shape[0], :] = ref[...].astype(F32)
            at += ref.shape[0]

        def clear(i, carry):
            z_ref[pl.ds(pl.multiple_of(i * 32, 32), 32), :] = jnp.zeros((32, double), F32)
            return carry

        lax.fori_loop(0, 2 * ROWS_Q // 32, clear, 0, unroll=6)
        place_rows(place_ref, me_ref, m_ref, z_ref, owners, local)

    return pl.pallas_call(
        kernel,
        out_shape=jax.ShapeDtypeStruct((2 * ROWS_Q, double), F32),
        in_specs=[smem()] * 2 + [vmem()] * n,
        out_specs=vmem(),
        scratch_shapes=[pltpu.VMEM((count, double), F32)],
        compiler_params=params(),
        name="place_first",
    )(places, me, *pieces)


def evaluate(t_ref, a_ref, cs_ref, start, points, width, write):
    chunk = math.gcd(points, 512)
    for at in range(0, points, chunk):
        here = slice(start + at, start + at + chunk)
        r = lax.dot_general(
            t_ref[...], a_ref[:, here], (((1,), (0,)), ((), ())), preferred_element_type=F32
        )
        total = r[:width]
        for k in range(1, KZ):
            lo = 2 * k * width
            total = total + r[lo : lo + width] * cs_ref[k : k + 1, here]
            total = total + r[lo + width : lo + 2 * width] * cs_ref[16 + k : 17 + k, here]
        write(slice(at, at + chunk), total)


def inverse_other(places, me, z, piece, a, cs, owners, local):
    double = piece.shape[1]
    width = double // 2
    points = a.shape[1] // 2

    def kernel(place_ref, me_ref, z_ref, piece_ref, a_ref, cs_ref, other_ref, t_ref, zz_ref, m_ref):
        m_ref[...] = piece_ref[...].astype(F32)
        place_rows(place_ref, me_ref, m_ref, zz_ref, owners, local)
        sign = sign_lanes(width)

        def combine(i, carry):
            base = pl.multiple_of(i * 32, 32)
            u, v = [], []
            for y in range(2):
                lo = base + 16 * y
                plus = zz_ref[pl.ds(lo, 8), :] + zz_ref[pl.ds(ROWS_Q + lo, 8), :]
                minus = zz_ref[pl.ds(lo + 8, 8), :] + zz_ref[pl.ds(ROWS_Q + lo + 8, 8), :]
                u.append(plus * sign + minus)
                v.append(pltpu.roll(plus - minus * sign, width, 1))
            zz_ref[pl.ds(base, 8), :] = u[0] + u[1]
            zz_ref[pl.ds(base + 8, 8), :] = v[1] - v[0]
            zz_ref[pl.ds(base + 16, 8), :] = -v[0] - v[1]
            zz_ref[pl.ds(base + 24, 8), :] = u[1] - u[0]
            return carry

        lax.fori_loop(0, KZ * GROUPS, combine, 0, unroll=9)
        for k in range(KZ):
            t_ref[k * double : (k + 1) * double, :] = zz_ref[
                k * ROWS_A : (k + 1) * ROWS_A, :
            ].T.astype(BF16)

        def write(here, total):
            other_ref[:, here] = total

        evaluate(t_ref, a_ref, cs_ref, points, points, width, write)

    return pl.pallas_call(
        kernel,
        out_shape=(
            jax.ShapeDtypeStruct((width, points), F32),
            jax.ShapeDtypeStruct((KZ * double, ROWS_A), BF16),
            jax.ShapeDtypeStruct(z.shape, F32),
        ),
        in_specs=[smem()] * 2 + [vmem()] * 4,
        out_specs=(vmem(), vmem(), vmem()),
        input_output_aliases={2: 2},
        scratch_shapes=[pltpu.VMEM(piece.shape, F32)],
        compiler_params=params(),
        name="inverse_other",
    )(places, me, z, piece, a, cs)[:2]


def inverse_own(t, a, cs, field, weight, bias):
    width, points = field.shape

    def kernel(t_ref, a_ref, cs_ref, field_ref, weight_ref, bias_ref, out_ref):
        def write(here, total):
            direct = lax.dot_general(
                weight_ref[...],
                field_ref[:, here],
                (((0,), (0,)), ((), ())),
                preferred_element_type=F32,
            )
            out_ref[:, here] = total + direct + bias_ref[...]

        evaluate(t_ref, a_ref, cs_ref, 0, points, width, write)

    return pl.pallas_call(
        kernel,
        out_shape=jax.ShapeDtypeStruct((width, points), F32),
        in_specs=[vmem()] * 6,
        out_specs=vmem(),
        compiler_params=params(),
        name="inverse_own",
    )(t, a, cs, field, weight, bias)


def finish(own, got):
    def kernel(own_ref, got_ref, out_ref):
        x = own_ref[...] + got_ref[...]
        out_ref[...] = (0.5 * x * (1.0 + lax.erf(x * math.sqrt(0.5)))).astype(BF16)

    return pl.pallas_call(
        kernel,
        out_shape=jax.ShapeDtypeStruct(own.shape, BF16),
        in_specs=[vmem()] * 2,
        out_specs=vmem(),
        compiler_params=params(),
        name="finish",
    )(own, got)


def body(coords, field, mode_list, spec_weight, bypass_weight, bypass_bias):
    width, points = field.shape
    modes_total = mode_list.shape[0]
    count = lax.axis_size("pts")
    bits = count.bit_length() - 1
    me = lax.axis_index("pts")
    local = modes_total // count
    norm = 1.0 / math.sqrt(points * count)
    scale = 1.0 / math.sqrt(modes_total)

    def swap(x, bit):
        return lax.ppermute(x, "pts", [(i, i ^ (1 << bit)) for i in range(count)])

    rows, flip = table_rows(mode_list)
    places = rows + jnp.where(flip, ROWS_Q, 0)
    signs = jnp.where(flip, -1.0, 1.0).astype(F32)
    my_signs = lax.dynamic_slice(signs, (me * local,), (local,)).reshape(1, local)
    me_array = jnp.full((1,), me, jnp.int32)
    owners = owners_of(count)
    near, far = owners[: count // 4], owners[count // 4 :]
    weights = jnp.transpose(spec_weight, (0, 2, 3, 4, 1))

    a, cs = make_tables(coords, swap(coords, 0))
    for depth in range(LAYERS):
        q, send = forward(rows, me_array, a, cs, field, swap(field, 0), norm, far, local)
        got = swap(send, 1)
        keep = keep_rows(rows, me_array, q, near, local)
        for bit in range(2, bits):
            half = keep.shape[0] // 2
            send = (keep[half:] + got[half:].astype(F32)).astype(BF16)
            keep = keep[:half] + got[:half].astype(F32)
            got = swap(send, bit)
        mixed = mix(keep, got, my_signs, weights, depth, scale)
        pieces = [mixed]
        for bit in range(bits - 1, 1, -1):
            pieces.append(swap(jnp.concatenate(pieces, 0), bit))
        last = swap(jnp.concatenate(pieces, 0), 1)
        z = place_first(places, me_array, pieces, near, local)
        theirs, t = inverse_other(places, me_array, z, last, a, cs, far, local)
        got = swap(theirs, 0)
        own = inverse_own(t, a, cs, field, bypass_weight[depth], bypass_bias[depth][:, None])
        field = finish(own, got)
    return field


def solution(mesh):
    placed = (
        P(None, ("group", "pts")),
        P(None, ("group", "pts")),
        P(),
        P(None, "pts", None, None, None),
        P(),
        P(),
    )
    return jax.shard_map(
        body, mesh=mesh, in_specs=placed, out_specs=P(None, ("group", "pts")), check_vma=False
    )
```

```python
import math

import jax
import jax.numpy as jnp
from jax import lax
from jax.experimental import pallas as pl
from jax.experimental.pallas import tpu as pltpu
from jax.sharding import PartitionSpec as P

KDIM = 16
GRID = 1024
LAYERS = 2
TWO_PI = 2.0 * math.pi
HALF = KDIM // 2
KZ = HALF + 1
GROUPS = HALF + 3
ROWS_A = GROUPS * 32
ROWS_Q = KZ * ROWS_A
VMEM = 24 * 1024 * 1024
F32 = jnp.float32
BF16 = jnp.bfloat16


def cost(microseconds):
    return pl.CostEstimate(flops=int(microseconds * 1.1e9), bytes_accessed=0, transcendentals=0)


def params():
    return pltpu.CompilerParams(vmem_limit_bytes=VMEM)


def vmem():
    return pl.BlockSpec(memory_space=pltpu.VMEM)


def smem():
    return pl.BlockSpec(memory_space=pltpu.SMEM)


def table_rows(mode_list):
    kx = mode_list // (KDIM * KDIM) - HALF
    ky = mode_list // KDIM % KDIM - HALF
    kz = mode_list % KDIM - HALF
    flip = kx < 0
    ky = jnp.where(flip, -ky, ky)
    kz = jnp.where(flip, -kz, kz)
    ax, ay, az = jnp.abs(kx), jnp.abs(ky), jnp.abs(kz)
    quarter = 2 * (ky < 0).astype(jnp.int32) + (kz < 0).astype(jnp.int32)
    group = jnp.where(ay < HALF, ax, jnp.where(ax < HALF, HALF + 1, HALF + 2))
    inner = jnp.where(ay < HALF, ay, jnp.where(ax < HALF, ax, 0))
    row = ((az * GROUPS + group) * 4 + quarter) * 8 + inner
    return row, flip


def tables_kernel(own_ref, other_ref, a_ref, cs_ref):
    points = jnp.concatenate([own_ref[...], other_ref[...]], 1)
    angle = points.astype(F32) * (TWO_PI / GRID)
    one_c, one_s = jnp.cos(angle), jnp.sin(angle)
    cos, sin = [jnp.ones_like(angle), one_c], [jnp.zeros_like(angle), one_s]
    for k in range(2, HALF + 1):
        i, j = k // 2, k - k // 2
        cos.append(cos[i] * cos[j] - sin[i] * sin[j])
        sin.append(sin[i] * cos[j] + cos[i] * sin[j])
    cx = jnp.concatenate([c[0:1] for c in cos[:HALF]], 0)
    sx = jnp.concatenate([s[0:1] for s in sin[:HALF]], 0)
    cy = jnp.concatenate([c[1:2] for c in cos[:HALF]], 0)
    sy = jnp.concatenate([s[1:2] for s in sin[:HALF]], 0)
    for g in range(GROUPS):
        if g <= HALF:
            c, s = cos[g][0:1], sin[g][0:1]
            parts = [c * cy, c * sy, s * cy, s * sy]
        elif g == HALF + 1:
            c, s = cos[HALF][1:2], sin[HALF][1:2]
            parts = [cx * c, cx * s, sx * c, sx * s]
        else:
            c, s = cos[HALF][1:2], sin[HALF][1:2]
            first = (lax.broadcasted_iota(jnp.int32, cx.shape, 0) == 0).astype(F32)
            cl, sl = first * cos[HALF][0:1], first * sin[HALF][0:1]
            parts = [cl * c, cl * s, sl * c, sl * s]
        a_ref[g * 32 : (g + 1) * 32, :] = jnp.concatenate(parts, 0).astype(BF16)
    pad = jnp.zeros((7, angle.shape[1]), F32)
    cs_ref[...] = jnp.concatenate(
        [c[2:3] for c in cos] + [pad] + [s[2:3] for s in sin] + [pad], 0
    )


def make_tables(own, other):
    points = 2 * own.shape[1]
    return pl.pallas_call(
        tables_kernel,
        out_shape=(
            jax.ShapeDtypeStruct((ROWS_A, points), BF16),
            jax.ShapeDtypeStruct((32, points), F32),
        ),
        in_specs=[vmem()] * 2,
        out_specs=(vmem(), vmem()),
        compiler_params=params(),
        cost_estimate=cost(1.2),
        name="tables",
    )(own, other)


def sign_lanes(width):
    lane = lax.broadcasted_iota(jnp.int32, (8, 2 * width), 1)
    return jnp.where(lane < width, 1.0, -1.0).astype(F32)


def owners_of(count):
    bits = count.bit_length() - 1
    return [
        sum(((t >> (bits - 2 - b)) & 1) << (b + 1) for b in range(bits - 1))
        for t in range(count // 2)
    ]


def spectrum(norm, a_ref, cs_ref, own_ref, other_ref, q_ref, hs_ref, b_refs):
    width, points = own_ref.shape
    hs_ref[:, :points] = own_ref[...].astype(F32) * norm
    hs_ref[:, points:] = other_ref[...].astype(F32) * norm

    def product(b):
        return lax.dot_general(
            a_ref[...], b, (((1,), (1,)), ((), ())), preferred_element_type=F32
        )

    first = product(hs_ref[...].astype(BF16))
    q_ref[0:ROWS_A, :] = jnp.concatenate([first, jnp.zeros_like(first)], 1)

    for pair in range(HALF // 2):
        b_ref = b_refs[pair % 2]
        for half in range(2):
            k = 2 * pair + 1 + half
            b_ref[2 * half * width : (2 * half + 1) * width, :] = (
                hs_ref[...] * cs_ref[k : k + 1, :]
            ).astype(BF16)
            b_ref[(2 * half + 1) * width : (2 * half + 2) * width, :] = (
                hs_ref[...] * cs_ref[16 + k : 17 + k, :]
            ).astype(BF16)
        both = product(b_ref[...])
        k = 2 * pair + 1
        q_ref[k * ROWS_A : (k + 1) * ROWS_A, :] = both[:, : 2 * width]
        q_ref[(k + 1) * ROWS_A : (k + 2) * ROWS_A, :] = both[:, 2 * width :]

    sign = sign_lanes(width)

    def combine(i, carry):
        base = pl.multiple_of(i * 32, 32)
        cc = q_ref[pl.ds(base, 8), :]
        cs = q_ref[pl.ds(base + 8, 8), :]
        sc = q_ref[pl.ds(base + 16, 8), :]
        ss = q_ref[pl.ds(base + 24, 8), :]
        for y in range(2):
            u = cc + ss if y else cc - ss
            v = pltpu.roll(sc - cs if y else sc + cs, width, 1)
            q_ref[pl.ds(base + 16 * y, 8), :] = u * sign - v
            q_ref[pl.ds(base + 16 * y + 8, 8), :] = u + v * sign
        return carry

    lax.fori_loop(0, KZ * GROUPS, combine, 0, unroll=9)


def gather_rows(row_ref, me_ref, q_ref, out_ref, owners, local):
    for at, owner in enumerate(owners):
        base = jnp.bitwise_xor(me_ref[0], owner) * local

        def step(j, carry, base=base, at=at):
            out_ref[pl.ds(at * local + j, 1), :] = q_ref[pl.ds(row_ref[base + j], 1), :]
            return carry

        lax.fori_loop(0, local, step, 0, unroll=32)


def forward(rows, me, a, cs, own, other, norm, first, second, local):
    width, points = own.shape
    shapes = [(len(owners) * local, 2 * width) for owners in (first, second)]

    def kernel(row_ref, me_ref, a_ref, cs_ref, own_ref, other_ref, q_ref, first_ref, second_ref, hs_ref, b0_ref, b1_ref, stage_ref):
        spectrum(norm, a_ref, cs_ref, own_ref, other_ref, q_ref, hs_ref, (b0_ref, b1_ref))
        gather_rows(row_ref, me_ref, q_ref, stage_ref, first + second, local)
        first_ref[...] = stage_ref[: shapes[0][0], :].astype(BF16)
        second_ref[...] = stage_ref[shapes[0][0] :, :].astype(BF16)

    return pl.pallas_call(
        kernel,
        out_shape=(
            jax.ShapeDtypeStruct((ROWS_Q, 2 * width), F32),
            jax.ShapeDtypeStruct(shapes[0], BF16),
            jax.ShapeDtypeStruct(shapes[1], BF16),
        ),
        in_specs=[smem()] * 2 + [vmem()] * 4,
        out_specs=(vmem(), vmem(), vmem()),
        scratch_shapes=[
            pltpu.VMEM((width, 2 * points), F32),
            pltpu.VMEM((4 * width, 2 * points), BF16),
            pltpu.VMEM((4 * width, 2 * points), BF16),
            pltpu.VMEM((shapes[0][0] + shapes[1][0], 2 * width), F32),
        ],
        compiler_params=params(),
        cost_estimate=cost(6.0),
        name="forward",
    )(rows, me, a, cs, own, other)


def keep_rows(rows, me, q, owners, local):
    def kernel(row_ref, me_ref, q_ref, out_ref):
        gather_rows(row_ref, me_ref, q_ref, out_ref, owners, local)

    return pl.pallas_call(
        kernel,
        out_shape=jax.ShapeDtypeStruct((len(owners) * local, q.shape[1]), F32),
        in_specs=[smem()] * 2 + [vmem()],
        out_specs=vmem(),
        compiler_params=params(),
        cost_estimate=cost(2.0),
        name="keep_rows",
    )(rows, me, q)


def merge(keep, got, count):
    rows = got.shape[0] // count

    def kernel(keep_ref, got_ref, *out_refs):
        for n, ref in enumerate(out_refs):
            here = slice(n * rows, (n + 1) * rows)
            total = keep_ref[rows + n * rows : 2 * rows + n * rows, :] + got_ref[here, :].astype(F32)
            ref[...] = total.astype(BF16)

    return pl.pallas_call(
        kernel,
        out_shape=(jax.ShapeDtypeStruct((rows, got.shape[1]), BF16),) * count,
        in_specs=[vmem()] * 2,
        out_specs=(vmem(),) * count,
        compiler_params=params(),
        cost_estimate=cost(0.3),
        name="merge",
    )(keep, got)


def mix(keep, gots, flip, weights, layer, scale):
    modes, double = flip.shape[1], keep.shape[1]
    width = double // 2
    block = 16

    def kernel(flip_ref, w_ref, keep_ref, *refs):
        got_refs, (out_ref, s_ref, acc_ref) = refs[:-3], refs[-3:]
        total = keep_ref[:modes, :]
        for ref in got_refs:
            total = total + ref[...].astype(F32)
        s_ref[...] = total.T
        s_ref[width:, :] = s_ref[width:, :] * flip_ref[...]

        for at in range(0, width, block):

            def add(i, carry, at=at):
                real, imag = carry
                re = s_ref[pl.ds(i, 1), :]
                im = s_ref[pl.ds(width + i, 1), :]
                wr = w_ref[layer, 0, i, at : at + block].astype(F32)
                wi = w_ref[layer, 1, i, at : at + block].astype(F32)
                return real + re * wr - im * wi, imag + re * wi + im * wr

            zero = jnp.zeros((block, modes), F32)
            real, imag = lax.fori_loop(0, width, add, (zero, zero), unroll=16)
            acc_ref[at : at + block, :] = real * scale
            acc_ref[width + at : width + at + block, :] = imag * (flip_ref[...] * scale)

        out_ref[...] = acc_ref[...].T.astype(BF16)

    return pl.pallas_call(
        kernel,
        out_shape=jax.ShapeDtypeStruct((modes, double), BF16),
        in_specs=[vmem()] * (3 + len(gots)),
        out_specs=vmem(),
        scratch_shapes=[pltpu.VMEM((double, modes), F32), pltpu.VMEM((double, modes), F32)],
        compiler_params=params(),
        cost_estimate=cost(1.8),
        name="mix",
    )(flip, weights, keep, *gots)


def place_rows(place_ref, me_ref, m_ref, z_ref, owners, local):
    for at, owner in enumerate(owners):
        base = jnp.bitwise_xor(me_ref[0], owner) * local

        def step(j, carry, base=base, at=at):
            z_ref[pl.ds(place_ref[base + j], 1), :] = m_ref[pl.ds(at * local + j, 1), :]
            return carry

        lax.fori_loop(0, local, step, 0, unroll=32)


def clear_table(double):
    def kernel(z_ref):
        def clear(i, carry):
            z_ref[pl.ds(pl.multiple_of(i * 32, 32), 32), :] = jnp.zeros((32, double), F32)
            return carry

        lax.fori_loop(0, 2 * ROWS_Q // 32, clear, 0, unroll=6)

    return pl.pallas_call(
        kernel,
        out_shape=jax.ShapeDtypeStruct((2 * ROWS_Q, double), F32),
        out_specs=vmem(),
        compiler_params=params(),
        cost_estimate=cost(0.8),
        name="clear_table",
    )()


def place_pieces(places, me, z, pieces, owners, local):
    double = pieces[0].shape[1]
    count = len(owners) * local
    n = len(pieces)

    def kernel(place_ref, me_ref, before_ref, *refs):
        z_ref, m_ref = refs[n:]
        at = 0
        for ref in refs[:n]:
            m_ref[at : at + ref.shape[0], :] = ref[...].astype(F32)
            at += ref.shape[0]
        place_rows(place_ref, me_ref, m_ref, z_ref, owners, local)

    return pl.pallas_call(
        kernel,
        out_shape=jax.ShapeDtypeStruct(z.shape, F32),
        in_specs=[smem()] * 2 + [vmem()] * (n + 1),
        out_specs=vmem(),
        input_output_aliases={2: 0},
        scratch_shapes=[pltpu.VMEM((count, double), F32)],
        compiler_params=params(),
        cost_estimate=cost(0.5 + 0.45 * count / 256),
        name="place_pieces",
    )(places, me, z, *pieces)


def evaluate(t_ref, a_ref, cs_ref, start, points, width, write):
    chunk = math.gcd(points, 512)
    for at in range(0, points, chunk):
        here = slice(start + at, start + at + chunk)
        r = lax.dot_general(
            t_ref[...], a_ref[:, here], (((1,), (0,)), ((), ())), preferred_element_type=F32
        )
        total = r[:width]
        for k in range(1, KZ):
            lo = 2 * k * width
            total = total + r[lo : lo + width] * cs_ref[k : k + 1, here]
            total = total + r[lo + width : lo + 2 * width] * cs_ref[16 + k : 17 + k, here]
        write(slice(at, at + chunk), total)


def inverse_other(places, me, z, piece, a, cs, owners, local):
    double = piece.shape[1]
    width = double // 2
    points = a.shape[1] // 2

    def kernel(place_ref, me_ref, z_ref, piece_ref, a_ref, cs_ref, other_ref, t_ref, zz_ref, m_ref):
        m_ref[...] = piece_ref[...].astype(F32)
        place_rows(place_ref, me_ref, m_ref, zz_ref, owners, local)
        sign = sign_lanes(width)

        def combine(i, carry):
            base = pl.multiple_of(i * 32, 32)
            u, v = [], []
            for y in range(2):
                lo = base + 16 * y
                plus = zz_ref[pl.ds(lo, 8), :] + zz_ref[pl.ds(ROWS_Q + lo, 8), :]
                minus = zz_ref[pl.ds(lo + 8, 8), :] + zz_ref[pl.ds(ROWS_Q + lo + 8, 8), :]
                u.append(plus * sign + minus)
                v.append(pltpu.roll(plus - minus * sign, width, 1))
            zz_ref[pl.ds(base, 8), :] = u[0] + u[1]
            zz_ref[pl.ds(base + 8, 8), :] = v[1] - v[0]
            zz_ref[pl.ds(base + 16, 8), :] = -v[0] - v[1]
            zz_ref[pl.ds(base + 24, 8), :] = u[1] - u[0]
            return carry

        lax.fori_loop(0, KZ * GROUPS, combine, 0, unroll=9)
        for k in range(KZ):
            t_ref[k * double : (k + 1) * double, :] = zz_ref[
                k * ROWS_A : (k + 1) * ROWS_A, :
            ].T.astype(BF16)

        def write(here, total):
            other_ref[:, here] = total

        evaluate(t_ref, a_ref, cs_ref, points, points, width, write)

    return pl.pallas_call(
        kernel,
        out_shape=(
            jax.ShapeDtypeStruct((width, points), F32),
            jax.ShapeDtypeStruct((KZ * double, ROWS_A), BF16),
            jax.ShapeDtypeStruct(z.shape, F32),
        ),
        in_specs=[smem()] * 2 + [vmem()] * 4,
        out_specs=(vmem(), vmem(), vmem()),
        input_output_aliases={2: 2},
        scratch_shapes=[pltpu.VMEM(piece.shape, F32)],
        compiler_params=params(),
        cost_estimate=cost(4.5),
        name="inverse_other",
    )(places, me, z, piece, a, cs)[:2]


def inverse_own(t, a, cs, field, weight, bias, layer):
    width, points = field.shape

    def kernel(t_ref, a_ref, cs_ref, field_ref, weight_ref, bias_ref, out_ref):
        diagonal = lax.broadcasted_iota(jnp.int32, (width, width), 0) == lax.broadcasted_iota(
            jnp.int32, (width, width), 1
        )
        row = bias_ref[layer : layer + 1, :]
        column = jnp.sum(jnp.where(diagonal, row, 0.0), axis=1, keepdims=True)

        def write(here, total):
            direct = lax.dot_general(
                weight_ref[layer],
                field_ref[:, here],
                (((0,), (0,)), ((), ())),
                preferred_element_type=F32,
            )
            out_ref[:, here] = total + direct + column

        evaluate(t_ref, a_ref, cs_ref, 0, points, width, write)

    return pl.pallas_call(
        kernel,
        out_shape=jax.ShapeDtypeStruct((width, points), F32),
        in_specs=[vmem()] * 6,
        out_specs=vmem(),
        compiler_params=params(),
        cost_estimate=cost(2.1),
        name="inverse_own",
    )(t, a, cs, field, weight, bias)


def finish(own, got):
    def kernel(own_ref, got_ref, out_ref):
        x = own_ref[...] + got_ref[...]
        out_ref[...] = (0.5 * x * (1.0 + lax.erf(x * math.sqrt(0.5)))).astype(BF16)

    return pl.pallas_call(
        kernel,
        out_shape=jax.ShapeDtypeStruct(own.shape, BF16),
        in_specs=[vmem()] * 2,
        out_specs=vmem(),
        compiler_params=params(),
        cost_estimate=cost(0.8),
        name="finish",
    )(own, got)


def body(coords, field, mode_list, spec_weight, bypass_weight, bypass_bias):
    width, points = field.shape
    modes_total = mode_list.shape[0]
    count = lax.axis_size("pts")
    bits = count.bit_length() - 1
    me = lax.axis_index("pts")
    local = modes_total // count
    norm = 1.0 / math.sqrt(points * count)
    scale = 1.0 / math.sqrt(modes_total)

    def swap(x, mask):
        return lax.ppermute(x, "pts", [(i, i ^ mask) for i in range(count)])

    rows, flip = table_rows(mode_list)
    places = rows + jnp.where(flip, ROWS_Q, 0)
    signs = jnp.where(flip, -1.0, 1.0).astype(F32)
    my_signs = lax.dynamic_slice(signs, (me * local,), (local,)).reshape(1, local)
    me_array = jnp.full((1,), me, jnp.int32)
    owners = owners_of(count)
    near, far = owners[: count // 4], owners[count // 4 :]
    weights = jnp.transpose(spec_weight, (0, 2, 3, 4, 1))

    quad = count // 8
    part = quad // 2 * local

    theirs = swap(field, 1)
    a, cs = make_tables(coords, swap(coords, 1))
    for depth in range(LAYERS):
        if depth:
            theirs = swap(field, 1)
        q, far_send, near_send = forward(
            rows, me_array, a, cs, field, theirs, norm, far[quad // 2 :], far[: quad // 2], local
        )
        far_got, near_got = swap(far_send, 2), swap(near_send, 2)
        keep = keep_rows(rows, me_array, q, near, local)
        sends = merge(keep, far_got, 3)
        gots = [near_got] + [swap(x, mask) for x, mask in zip(sends, (8, 4, 12))]
        for bit in range(4, bits):
            total = keep[:part] if bit == 4 else keep
            for got in gots:
                total = total + got.astype(F32)
            half = total.shape[0] // 2
            keep = total[:half]
            gots = [swap(total[half:].astype(BF16), 1 << bit)]
        pieces = mix(keep, gots, my_signs, weights, depth, scale)
        z = clear_table(2 * width)
        for bit in range(bits - 1, 3, -1):
            pieces = jnp.concatenate([pieces, swap(pieces, 1 << bit)], 0)
        over = swap(pieces, 8)
        z = place_pieces(places, me_array, z, [pieces], near[: quad // 2], local)
        pieces = jnp.concatenate([pieces, over], 0)
        across, far_first = swap(pieces, 4), swap(pieces, 2)
        z = place_pieces(places, me_array, z, [over], near[quad // 2 : quad], local)
        last = swap(across, 2)
        z = place_pieces(
            places, me_array, z, [across, far_first], near[quad:] + far[:quad], local
        )
        theirs, t = inverse_other(places, me_array, z, last, a, cs, far[quad:], local)
        got = swap(theirs, 1)
        own = inverse_own(t, a, cs, field, bypass_weight, bypass_bias, depth)
        field = finish(own, got)
    return field


def solution(mesh):
    placed = (
        P(None, ("group", "pts")),
        P(None, ("group", "pts")),
        P(),
        P(None, "pts", None, None, None),
        P(),
        P(),
    )
    return jax.shard_map(
        body, mesh=mesh, in_specs=placed, out_specs=P(None, ("group", "pts")), check_vma=False
    )
```

```python
import math

import jax
import jax.numpy as jnp
from jax import lax
from jax.experimental import pallas as pl
from jax.experimental.pallas import tpu as pltpu
from jax.sharding import PartitionSpec as P

KDIM = 16
GRID = 1024
LAYERS = 2
TWO_PI = 2.0 * math.pi
HALF = KDIM // 2
KZ = HALF + 1
GROUPS = HALF + 3
ROWS_A = GROUPS * 32
ROWS_Q = KZ * ROWS_A
VMEM = 24 * 1024 * 1024
F32 = jnp.float32
BF16 = jnp.bfloat16


def cost(microseconds):
    return pl.CostEstimate(flops=int(microseconds * 1.1e9), bytes_accessed=0, transcendentals=0)


def params():
    return pltpu.CompilerParams(vmem_limit_bytes=VMEM)


def vmem():
    return pl.BlockSpec(memory_space=pltpu.VMEM)


def smem():
    return pl.BlockSpec(memory_space=pltpu.SMEM)


def table_rows(mode_list):
    kx = mode_list // (KDIM * KDIM) - HALF
    ky = mode_list // KDIM % KDIM - HALF
    kz = mode_list % KDIM - HALF
    flip = kx < 0
    ky = jnp.where(flip, -ky, ky)
    kz = jnp.where(flip, -kz, kz)
    ax, ay, az = jnp.abs(kx), jnp.abs(ky), jnp.abs(kz)
    quarter = 2 * (ky < 0).astype(jnp.int32) + (kz < 0).astype(jnp.int32)
    group = jnp.where(ay < HALF, ax, jnp.where(ax < HALF, HALF + 1, HALF + 2))
    inner = jnp.where(ay < HALF, ay, jnp.where(ax < HALF, ax, 0))
    row = ((az * GROUPS + group) * 4 + quarter) * 8 + inner
    return row, flip


def tables_kernel(own_ref, other_ref, a_ref, cs_ref):
    points = jnp.concatenate([own_ref[...], other_ref[...]], 1)
    angle = points.astype(F32) * (TWO_PI / GRID)
    one_c, one_s = jnp.cos(angle), jnp.sin(angle)
    cos, sin = [jnp.ones_like(angle), one_c], [jnp.zeros_like(angle), one_s]
    for k in range(2, HALF + 1):
        i, j = k // 2, k - k // 2
        cos.append(cos[i] * cos[j] - sin[i] * sin[j])
        sin.append(sin[i] * cos[j] + cos[i] * sin[j])
    cx = jnp.concatenate([c[0:1] for c in cos[:HALF]], 0)
    sx = jnp.concatenate([s[0:1] for s in sin[:HALF]], 0)
    cy = jnp.concatenate([c[1:2] for c in cos[:HALF]], 0)
    sy = jnp.concatenate([s[1:2] for s in sin[:HALF]], 0)
    for g in range(GROUPS):
        if g <= HALF:
            c, s = cos[g][0:1], sin[g][0:1]
            parts = [c * cy, c * sy, s * cy, s * sy]
        elif g == HALF + 1:
            c, s = cos[HALF][1:2], sin[HALF][1:2]
            parts = [cx * c, cx * s, sx * c, sx * s]
        else:
            c, s = cos[HALF][1:2], sin[HALF][1:2]
            first = (lax.broadcasted_iota(jnp.int32, cx.shape, 0) == 0).astype(F32)
            cl, sl = first * cos[HALF][0:1], first * sin[HALF][0:1]
            parts = [cl * c, cl * s, sl * c, sl * s]
        a_ref[g * 32 : (g + 1) * 32, :] = jnp.concatenate(parts, 0).astype(BF16)
    pad = jnp.zeros((7, angle.shape[1]), F32)
    cs_ref[...] = jnp.concatenate(
        [c[2:3] for c in cos] + [pad] + [s[2:3] for s in sin] + [pad], 0
    )


def make_tables(own, other):
    points = 2 * own.shape[1]
    return pl.pallas_call(
        tables_kernel,
        out_shape=(
            jax.ShapeDtypeStruct((ROWS_A, points), BF16),
            jax.ShapeDtypeStruct((32, points), F32),
        ),
        in_specs=[vmem()] * 2,
        out_specs=(vmem(), vmem()),
        compiler_params=params(),
        cost_estimate=cost(1.2),
        name="tables",
    )(own, other)


def sign_lanes(width):
    lane = lax.broadcasted_iota(jnp.int32, (8, 2 * width), 1)
    return jnp.where(lane < width, 1.0, -1.0).astype(F32)


def owners_of(count):
    bits = count.bit_length() - 1
    return [
        sum(((t >> (bits - 2 - b)) & 1) << (b + 1) for b in range(bits - 1))
        for t in range(count // 2)
    ]


def spectrum(norm, a_ref, cs_ref, own_ref, other_ref, q_ref, hs_ref, b_refs):
    width, points = own_ref.shape
    hs_ref[:, :points] = own_ref[...].astype(F32) * norm
    hs_ref[:, points:] = other_ref[...].astype(F32) * norm

    def product(b):
        return lax.dot_general(
            a_ref[...], b, (((1,), (1,)), ((), ())), preferred_element_type=F32
        )

    first = product(hs_ref[...].astype(BF16))
    q_ref[0:ROWS_A, :] = jnp.concatenate([first, jnp.zeros_like(first)], 1)

    for pair in range(HALF // 2):
        b_ref = b_refs[pair % 2]
        for half in range(2):
            k = 2 * pair + 1 + half
            b_ref[2 * half * width : (2 * half + 1) * width, :] = (
                hs_ref[...] * cs_ref[k : k + 1, :]
            ).astype(BF16)
            b_ref[(2 * half + 1) * width : (2 * half + 2) * width, :] = (
                hs_ref[...] * cs_ref[16 + k : 17 + k, :]
            ).astype(BF16)
        both = product(b_ref[...])
        k = 2 * pair + 1
        q_ref[k * ROWS_A : (k + 1) * ROWS_A, :] = both[:, : 2 * width]
        q_ref[(k + 1) * ROWS_A : (k + 2) * ROWS_A, :] = both[:, 2 * width :]

    sign = sign_lanes(width)

    def combine(i, carry):
        base = pl.multiple_of(i * 32, 32)
        cc = q_ref[pl.ds(base, 8), :]
        cs = q_ref[pl.ds(base + 8, 8), :]
        sc = q_ref[pl.ds(base + 16, 8), :]
        ss = q_ref[pl.ds(base + 24, 8), :]
        for y in range(2):
            u = cc + ss if y else cc - ss
            v = pltpu.roll(sc - cs if y else sc + cs, width, 1)
            q_ref[pl.ds(base + 16 * y, 8), :] = u * sign - v
            q_ref[pl.ds(base + 16 * y + 8, 8), :] = u + v * sign
        return carry

    lax.fori_loop(0, KZ * GROUPS, combine, 0, unroll=9)


def gather_rows(row_ref, me_ref, q_ref, out_ref, owners, local):
    for at, owner in enumerate(owners):
        base = jnp.bitwise_xor(me_ref[0], owner) * local

        def step(j, carry, base=base, at=at):
            out_ref[pl.ds(at * local + j, 1), :] = q_ref[pl.ds(row_ref[base + j], 1), :]
            return carry

        lax.fori_loop(0, local, step, 0, unroll=32)


def forward(rows, me, a, cs, own, other, norm, lists, local):
    width, points = own.shape
    sizes = [len(owners) * local for owners in lists]

    def kernel(row_ref, me_ref, a_ref, cs_ref, own_ref, other_ref, q_ref, *refs):
        send_refs, (hs_ref, b0_ref, b1_ref, stage_ref) = refs[:-4], refs[-4:]
        spectrum(norm, a_ref, cs_ref, own_ref, other_ref, q_ref, hs_ref, (b0_ref, b1_ref))
        gather_rows(row_ref, me_ref, q_ref, stage_ref, sum(lists, []), local)
        at = 0
        for ref in send_refs:
            ref[...] = stage_ref[at : at + ref.shape[0], :].astype(BF16)
            at += ref.shape[0]

    return pl.pallas_call(
        kernel,
        out_shape=(jax.ShapeDtypeStruct((ROWS_Q, 2 * width), F32),)
        + tuple(jax.ShapeDtypeStruct((size, 2 * width), BF16) for size in sizes),
        in_specs=[smem()] * 2 + [vmem()] * 4,
        out_specs=(vmem(),) * (1 + len(sizes)),
        scratch_shapes=[
            pltpu.VMEM((width, 2 * points), F32),
            pltpu.VMEM((4 * width, 2 * points), BF16),
            pltpu.VMEM((4 * width, 2 * points), BF16),
            pltpu.VMEM((sum(sizes), 2 * width), F32),
        ],
        compiler_params=params(),
        cost_estimate=cost(6.0),
        name="forward",
    )(rows, me, a, cs, own, other)


def keep_rows(rows, me, q, owners, local):
    def kernel(row_ref, me_ref, q_ref, out_ref):
        gather_rows(row_ref, me_ref, q_ref, out_ref, owners, local)

    return pl.pallas_call(
        kernel,
        out_shape=jax.ShapeDtypeStruct((len(owners) * local, q.shape[1]), F32),
        in_specs=[smem()] * 2 + [vmem()],
        out_specs=vmem(),
        compiler_params=params(),
        cost_estimate=cost(2.0),
        name="keep_rows",
    )(rows, me, q)


def merge(keep, got, keep_at, got_at, rows):
    def kernel(keep_ref, got_ref, out_ref):
        total = keep_ref[keep_at : keep_at + rows, :]
        total = total + got_ref[got_at : got_at + rows, :].astype(F32)
        out_ref[...] = total.astype(BF16)

    return pl.pallas_call(
        kernel,
        out_shape=jax.ShapeDtypeStruct((rows, got.shape[1]), BF16),
        in_specs=[vmem()] * 2,
        out_specs=vmem(),
        compiler_params=params(),
        cost_estimate=cost(0.2),
        name="merge",
    )(keep, got)


def mix(keep, gots, flip, weights, layer, scale):
    modes, double = flip.shape[1], keep.shape[1]
    width = double // 2
    block = 16

    def kernel(flip_ref, w_ref, keep_ref, *refs):
        got_refs, (out_ref, s_ref, acc_ref) = refs[:-3], refs[-3:]
        total = keep_ref[:modes, :]
        for ref in got_refs:
            total = total + ref[:modes, :].astype(F32)
        s_ref[...] = total.T
        s_ref[width:, :] = s_ref[width:, :] * flip_ref[...]

        for at in range(0, width, block):

            def add(i, carry, at=at):
                real, imag = carry
                re = s_ref[pl.ds(i, 1), :]
                im = s_ref[pl.ds(width + i, 1), :]
                wr = w_ref[layer, 0, i, at : at + block].astype(F32)
                wi = w_ref[layer, 1, i, at : at + block].astype(F32)
                return real + re * wr - im * wi, imag + re * wi + im * wr

            zero = jnp.zeros((block, modes), F32)
            real, imag = lax.fori_loop(0, width, add, (zero, zero), unroll=16)
            acc_ref[at : at + block, :] = real * scale
            acc_ref[width + at : width + at + block, :] = imag * (flip_ref[...] * scale)

        out_ref[...] = acc_ref[...].T.astype(BF16)

    return pl.pallas_call(
        kernel,
        out_shape=jax.ShapeDtypeStruct((modes, double), BF16),
        in_specs=[vmem()] * (3 + len(gots)),
        out_specs=vmem(),
        scratch_shapes=[pltpu.VMEM((double, modes), F32), pltpu.VMEM((double, modes), F32)],
        compiler_params=params(),
        cost_estimate=cost(1.8),
        name="mix",
    )(flip, weights, keep, *gots)


def place_rows(place_ref, me_ref, m_ref, z_ref, owners, local):
    for at, owner in enumerate(owners):
        base = jnp.bitwise_xor(me_ref[0], owner) * local

        def step(j, carry, base=base, at=at):
            z_ref[pl.ds(place_ref[base + j], 1), :] = m_ref[pl.ds(at * local + j, 1), :]
            return carry

        lax.fori_loop(0, local, step, 0, unroll=32)


def clear_table(double):
    def kernel(z_ref):
        def clear(i, carry):
            z_ref[pl.ds(pl.multiple_of(i * 32, 32), 32), :] = jnp.zeros((32, double), F32)
            return carry

        lax.fori_loop(0, 2 * ROWS_Q // 32, clear, 0, unroll=6)

    return pl.pallas_call(
        kernel,
        out_shape=jax.ShapeDtypeStruct((2 * ROWS_Q, double), F32),
        out_specs=vmem(),
        compiler_params=params(),
        cost_estimate=cost(0.8),
        name="clear_table",
    )()


def place_pieces(places, me, z, pieces, owners, local):
    double = pieces[0].shape[1]
    count = len(owners) * local
    n = len(pieces)

    def kernel(place_ref, me_ref, before_ref, *refs):
        z_ref, m_ref = refs[n:]
        at = 0
        for ref in refs[:n]:
            m_ref[at : at + ref.shape[0], :] = ref[...].astype(F32)
            at += ref.shape[0]
        place_rows(place_ref, me_ref, m_ref, z_ref, owners, local)

    return pl.pallas_call(
        kernel,
        out_shape=jax.ShapeDtypeStruct(z.shape, F32),
        in_specs=[smem()] * 2 + [vmem()] * (n + 1),
        out_specs=vmem(),
        input_output_aliases={2: 0},
        scratch_shapes=[pltpu.VMEM((count, double), F32)],
        compiler_params=params(),
        cost_estimate=cost(0.5 + 0.45 * count / 256),
        name="place_pieces",
    )(places, me, z, *pieces)


def evaluate(t_ref, a_ref, cs_ref, start, points, width, write):
    chunk = math.gcd(points, 512)
    for at in range(0, points, chunk):
        here = slice(start + at, start + at + chunk)
        r = lax.dot_general(
            t_ref[...], a_ref[:, here], (((1,), (0,)), ((), ())), preferred_element_type=F32
        )
        total = r[:width]
        for k in range(1, KZ):
            lo = 2 * k * width
            total = total + r[lo : lo + width] * cs_ref[k : k + 1, here]
            total = total + r[lo + width : lo + 2 * width] * cs_ref[16 + k : 17 + k, here]
        write(slice(at, at + chunk), total)


def inverse_other(places, me, z, piece, a, cs, owners, local):
    double = piece.shape[1]
    width = double // 2
    points = a.shape[1] // 2

    def kernel(place_ref, me_ref, z_ref, piece_ref, a_ref, cs_ref, other_ref, t_ref, zz_ref, m_ref):
        m_ref[...] = piece_ref[...].astype(F32)
        place_rows(place_ref, me_ref, m_ref, zz_ref, owners, local)
        sign = sign_lanes(width)

        def combine(i, carry):
            base = pl.multiple_of(i * 32, 32)
            u, v = [], []
            for y in range(2):
                lo = base + 16 * y
                plus = zz_ref[pl.ds(lo, 8), :] + zz_ref[pl.ds(ROWS_Q + lo, 8), :]
                minus = zz_ref[pl.ds(lo + 8, 8), :] + zz_ref[pl.ds(ROWS_Q + lo + 8, 8), :]
                u.append(plus * sign + minus)
                v.append(pltpu.roll(plus - minus * sign, width, 1))
            zz_ref[pl.ds(base, 8), :] = u[0] + u[1]
            zz_ref[pl.ds(base + 8, 8), :] = v[1] - v[0]
            zz_ref[pl.ds(base + 16, 8), :] = -v[0] - v[1]
            zz_ref[pl.ds(base + 24, 8), :] = u[1] - u[0]
            return carry

        lax.fori_loop(0, KZ * GROUPS, combine, 0, unroll=9)
        for k in range(KZ):
            t_ref[k * double : (k + 1) * double, :] = zz_ref[
                k * ROWS_A : (k + 1) * ROWS_A, :
            ].T.astype(BF16)

        def write(here, total):
            other_ref[:, here] = total

        evaluate(t_ref, a_ref, cs_ref, points, points, width, write)

    return pl.pallas_call(
        kernel,
        out_shape=(
            jax.ShapeDtypeStruct((width, points), F32),
            jax.ShapeDtypeStruct((KZ * double, ROWS_A), BF16),
            jax.ShapeDtypeStruct(z.shape, F32),
        ),
        in_specs=[smem()] * 2 + [vmem()] * 4,
        out_specs=(vmem(), vmem(), vmem()),
        input_output_aliases={2: 2},
        scratch_shapes=[pltpu.VMEM(piece.shape, F32)],
        compiler_params=params(),
        cost_estimate=cost(4.5),
        name="inverse_other",
    )(places, me, z, piece, a, cs)[:2]


def inverse_own(t, a, cs, field, weight, bias, layer):
    width, points = field.shape

    def kernel(t_ref, a_ref, cs_ref, field_ref, weight_ref, bias_ref, out_ref):
        diagonal = lax.broadcasted_iota(jnp.int32, (width, width), 0) == lax.broadcasted_iota(
            jnp.int32, (width, width), 1
        )
        row = bias_ref[layer : layer + 1, :]
        column = jnp.sum(jnp.where(diagonal, row, 0.0), axis=1, keepdims=True)

        def write(here, total):
            direct = lax.dot_general(
                weight_ref[layer],
                field_ref[:, here],
                (((0,), (0,)), ((), ())),
                preferred_element_type=F32,
            )
            out_ref[:, here] = total + direct + column

        evaluate(t_ref, a_ref, cs_ref, 0, points, width, write)

    return pl.pallas_call(
        kernel,
        out_shape=jax.ShapeDtypeStruct((width, points), F32),
        in_specs=[vmem()] * 6,
        out_specs=vmem(),
        compiler_params=params(),
        cost_estimate=cost(2.1),
        name="inverse_own",
    )(t, a, cs, field, weight, bias)


def finish(own, got):
    def kernel(own_ref, got_ref, out_ref):
        x = own_ref[...] + got_ref[...]
        out_ref[...] = (0.5 * x * (1.0 + lax.erf(x * math.sqrt(0.5)))).astype(BF16)

    return pl.pallas_call(
        kernel,
        out_shape=jax.ShapeDtypeStruct(own.shape, BF16),
        in_specs=[vmem()] * 2,
        out_specs=vmem(),
        compiler_params=params(),
        cost_estimate=cost(0.8),
        name="finish",
    )(own, got)


def body(coords, field, mode_list, spec_weight, bypass_weight, bypass_bias):
    width, points = field.shape
    modes_total = mode_list.shape[0]
    count = lax.axis_size("pts")
    bits = count.bit_length() - 1
    me = lax.axis_index("pts")
    local = modes_total // count
    norm = 1.0 / math.sqrt(points * count)
    scale = 1.0 / math.sqrt(modes_total)

    def swap(x, mask):
        return lax.ppermute(x, "pts", [(i, i ^ mask) for i in range(count)])

    rows, flip = table_rows(mode_list)
    places = rows + jnp.where(flip, ROWS_Q, 0)
    signs = jnp.where(flip, -1.0, 1.0).astype(F32)
    my_signs = lax.dynamic_slice(signs, (me * local,), (local,)).reshape(1, local)
    me_array = jnp.full((1,), me, jnp.int32)
    owners = owners_of(count)
    near, far = owners[: count // 4], owners[count // 4 :]
    weights = jnp.transpose(spec_weight, (0, 2, 3, 4, 1))

    quarter = count // 16
    part = quarter * local
    near = [near[n * quarter : (n + 1) * quarter] for n in range(4)]
    far = [far[n * quarter : (n + 1) * quarter] for n in range(4)]

    theirs = swap(field, 1)
    a, cs = make_tables(coords, swap(coords, 1))
    for depth in range(LAYERS):
        if depth:
            theirs = swap(field, 1)
        q, send_both, send_three, send_rest = forward(
            rows, me_array, a, cs, field, theirs, norm,
            [far[3], far[1], far[0] + far[2]], local,
        )
        got_both, got_three, got_rest = (swap(x, 2) for x in (send_both, send_three, send_rest))
        keep = keep_rows(rows, me_array, q, near[0] + near[1] + near[2] + near[3], local)
        gots = [
            swap(merge(keep, got_both, 3 * part, 0, part), 12),
            swap(merge(keep, got_three, part, 0, part), 8),
            swap(merge(keep, got_rest, 2 * part, part, part), 4),
            got_rest,
        ]
        for bit in range(4, bits):
            total = keep[:part] if bit == 4 else keep
            for got in gots:
                total = total + got[: total.shape[0]].astype(F32)
            half = total.shape[0] // 2
            keep = total[:half]
            gots = [swap(total[half:].astype(BF16), 1 << bit)]
        pieces = mix(keep, gots, my_signs, weights, depth, scale)
        z = clear_table(2 * width)
        for bit in range(bits - 1, 3, -1):
            pieces = jnp.concatenate([pieces, swap(pieces, 1 << bit)], 0)
        over = [swap(pieces, mask) for mask in (8, 12, 4)]
        far_first = swap(pieces, 2)
        far_next = swap(jnp.concatenate(over[:2], 0), 2)
        last = swap(over[2], 2)
        z = place_pieces(places, me_array, z, [pieces], near[0], local)
        z = place_pieces(
            places, me_array, z, [far_first] + over, far[0] + near[1] + near[3] + near[2], local
        )
        z = place_pieces(places, me_array, z, [far_next], far[1] + far[3], local)
        theirs, t = inverse_other(places, me_array, z, last, a, cs, far[2], local)
        got = swap(theirs, 1)
        own = inverse_own(t, a, cs, field, bypass_weight, bypass_bias, depth)
        field = finish(own, got)
    return field


def solution(mesh):
    placed = (
        P(None, ("group", "pts")),
        P(None, ("group", "pts")),
        P(),
        P(None, "pts", None, None, None),
        P(),
        P(),
    )
    return jax.shard_map(
        body, mesh=mesh, in_specs=placed, out_specs=P(None, ("group", "pts")), check_vma=False
    )
```

```python
import math

import jax
import jax.numpy as jnp
from jax import lax
from jax.experimental import pallas as pl
from jax.experimental.pallas import tpu as pltpu
from jax.sharding import PartitionSpec as P

KDIM = 16
GRID = 1024
LAYERS = 2
TWO_PI = 2.0 * math.pi
HALF = KDIM // 2
KZ = HALF + 1
GROUPS = HALF + 3
ROWS_A = GROUPS * 32
ROWS_Q = KZ * ROWS_A
VMEM = 24 * 1024 * 1024
F32 = jnp.float32
BF16 = jnp.bfloat16


def cost(microseconds):
    return pl.CostEstimate(flops=int(microseconds * 1.1e9), bytes_accessed=0, transcendentals=0)


def params():
    return pltpu.CompilerParams(vmem_limit_bytes=VMEM)


def vmem():
    return pl.BlockSpec(memory_space=pltpu.VMEM)


def smem():
    return pl.BlockSpec(memory_space=pltpu.SMEM)


def table_rows(mode_list):
    kx = mode_list // (KDIM * KDIM) - HALF
    ky = mode_list // KDIM % KDIM - HALF
    kz = mode_list % KDIM - HALF
    flip = kx < 0
    ky = jnp.where(flip, -ky, ky)
    kz = jnp.where(flip, -kz, kz)
    ax, ay, az = jnp.abs(kx), jnp.abs(ky), jnp.abs(kz)
    quarter = 2 * (ky < 0).astype(jnp.int32) + (kz < 0).astype(jnp.int32)
    group = jnp.where(ay < HALF, ax, jnp.where(ax < HALF, HALF + 1, HALF + 2))
    inner = jnp.where(ay < HALF, ay, jnp.where(ax < HALF, ax, 0))
    row = ((az * GROUPS + group) * 4 + quarter) * 8 + inner
    return row, flip


def tables_kernel(own_ref, other_ref, a_ref, cs_ref):
    points = jnp.concatenate([own_ref[...], other_ref[...]], 1)
    angle = points.astype(F32) * (TWO_PI / GRID)
    one_c, one_s = jnp.cos(angle), jnp.sin(angle)
    cos, sin = [jnp.ones_like(angle), one_c], [jnp.zeros_like(angle), one_s]
    for k in range(2, HALF + 1):
        i, j = k // 2, k - k // 2
        cos.append(cos[i] * cos[j] - sin[i] * sin[j])
        sin.append(sin[i] * cos[j] + cos[i] * sin[j])
    cx = jnp.concatenate([c[0:1] for c in cos[:HALF]], 0)
    sx = jnp.concatenate([s[0:1] for s in sin[:HALF]], 0)
    cy = jnp.concatenate([c[1:2] for c in cos[:HALF]], 0)
    sy = jnp.concatenate([s[1:2] for s in sin[:HALF]], 0)
    for g in range(GROUPS):
        if g <= HALF:
            c, s = cos[g][0:1], sin[g][0:1]
            parts = [c * cy, c * sy, s * cy, s * sy]
        elif g == HALF + 1:
            c, s = cos[HALF][1:2], sin[HALF][1:2]
            parts = [cx * c, cx * s, sx * c, sx * s]
        else:
            c, s = cos[HALF][1:2], sin[HALF][1:2]
            first = (lax.broadcasted_iota(jnp.int32, cx.shape, 0) == 0).astype(F32)
            cl, sl = first * cos[HALF][0:1], first * sin[HALF][0:1]
            parts = [cl * c, cl * s, sl * c, sl * s]
        a_ref[g * 32 : (g + 1) * 32, :] = jnp.concatenate(parts, 0).astype(BF16)
    pad = jnp.zeros((7, angle.shape[1]), F32)
    cs_ref[...] = jnp.concatenate(
        [c[2:3] for c in cos] + [pad] + [s[2:3] for s in sin] + [pad], 0
    )


def make_tables(own, other):
    points = 2 * own.shape[1]
    return pl.pallas_call(
        tables_kernel,
        out_shape=(
            jax.ShapeDtypeStruct((ROWS_A, points), BF16),
            jax.ShapeDtypeStruct((32, points), F32),
        ),
        in_specs=[vmem()] * 2,
        out_specs=(vmem(), vmem()),
        compiler_params=params(),
        cost_estimate=cost(1.2),
        name="tables",
    )(own, other)


def sign_lanes(width):
    lane = lax.broadcasted_iota(jnp.int32, (8, 2 * width), 1)
    return jnp.where(lane < width, 1.0, -1.0).astype(F32)


def owners_of(count):
    bits = count.bit_length() - 1
    return [
        sum(((t >> (bits - 2 - b)) & 1) << (b + 1) for b in range(bits - 1))
        for t in range(count // 2)
    ]


def sums(norm, half, a_ref, cs_ref, h_ref, hs_ref, b_refs, write):
    width, points = h_ref.shape
    here = slice(half * points, (half + 1) * points)
    hs_ref[...] = h_ref[...].astype(F32) * norm

    def product(b):
        return lax.dot_general(
            a_ref[:, here], b, (((1,), (1,)), ((), ())), preferred_element_type=F32
        )

    first = product(hs_ref[...].astype(BF16))
    write(0, jnp.concatenate([first, jnp.zeros_like(first)], 1))
    for pair in range(HALF // 2):
        b_ref = b_refs[pair % 2]
        for part in range(2):
            k = 2 * pair + 1 + part
            b_ref[2 * part * width : (2 * part + 1) * width, :] = (
                hs_ref[...] * cs_ref[k : k + 1, here]
            ).astype(BF16)
            b_ref[(2 * part + 1) * width : (2 * part + 2) * width, :] = (
                hs_ref[...] * cs_ref[16 + k : 17 + k, here]
            ).astype(BF16)
        both = product(b_ref[...])
        write(2 * pair + 1, both[:, : 2 * width])
        write(2 * pair + 2, both[:, 2 * width :])


def combine_rows(q_ref, width):
    sign = sign_lanes(width)

    def combine(i, carry):
        base = pl.multiple_of(i * 32, 32)
        cc = q_ref[pl.ds(base, 8), :]
        cs = q_ref[pl.ds(base + 8, 8), :]
        sc = q_ref[pl.ds(base + 16, 8), :]
        ss = q_ref[pl.ds(base + 24, 8), :]
        for y in range(2):
            u = cc + ss if y else cc - ss
            v = pltpu.roll(sc - cs if y else sc + cs, width, 1)
            q_ref[pl.ds(base + 16 * y, 8), :] = u * sign - v
            q_ref[pl.ds(base + 16 * y + 8, 8), :] = u + v * sign
        return carry

    lax.fori_loop(0, KZ * GROUPS, combine, 0, unroll=9)


def sum_scratch(width, points):
    return [
        pltpu.VMEM((width, points), F32),
        pltpu.VMEM((4 * width, points), BF16),
        pltpu.VMEM((4 * width, points), BF16),
    ]


def forward_own(a, cs, own, norm):
    width, points = own.shape

    def kernel(a_ref, cs_ref, own_ref, q_ref, hs_ref, b0_ref, b1_ref):
        def write(k, total):
            q_ref[k * ROWS_A : (k + 1) * ROWS_A, :] = total

        sums(norm, 0, a_ref, cs_ref, own_ref, hs_ref, (b0_ref, b1_ref), write)

    return pl.pallas_call(
        kernel,
        out_shape=jax.ShapeDtypeStruct((ROWS_Q, 2 * width), F32),
        in_specs=[vmem()] * 3,
        out_specs=vmem(),
        scratch_shapes=sum_scratch(width, points),
        compiler_params=params(),
        cost_estimate=cost(2.0),
        name="forward_own",
    )(a, cs, own)


def gather_rows(row_ref, q_ref, out_ref, owners, local):
    me = lax.axis_index("pts")
    for at, owner in enumerate(owners):
        base = jnp.bitwise_xor(me, owner) * local

        def step(j, carry, base=base, at=at):
            out_ref[pl.ds(at * local + j, 1), :] = q_ref[pl.ds(row_ref[base + j], 1), :]
            return carry

        lax.fori_loop(0, local, step, 0, unroll=32)


def forward(rows, a, cs, q, other, norm, lists, local):
    width, points = other.shape
    sizes = [len(owners) * local for owners in lists]

    def kernel(list_ref, a_ref, cs_ref, before_ref, other_ref, q_ref, *refs):
        send_refs, (hs_ref, b0_ref, b1_ref, stage_ref, row_ref, sem) = refs[:-6], refs[-6:]
        copy = pltpu.make_async_copy(list_ref, row_ref, sem)
        copy.start()

        def write(k, total):
            here = slice(k * ROWS_A, (k + 1) * ROWS_A)
            q_ref[here, :] = before_ref[here, :] + total

        sums(norm, 1, a_ref, cs_ref, other_ref, hs_ref, (b0_ref, b1_ref), write)
        combine_rows(q_ref, width)
        copy.wait()
        gather_rows(row_ref, q_ref, stage_ref, sum(lists, []), local)
        at = 0
        for ref in send_refs:
            ref[...] = stage_ref[at : at + ref.shape[0], :].astype(BF16)
            at += ref.shape[0]

    return pl.pallas_call(
        kernel,
        out_shape=(jax.ShapeDtypeStruct((ROWS_Q, 2 * width), F32),)
        + tuple(jax.ShapeDtypeStruct((size, 2 * width), BF16) for size in sizes),
        in_specs=[pl.BlockSpec(memory_space=pl.ANY)] + [vmem()] * 4,
        out_specs=(vmem(),) * (1 + len(sizes)),
        scratch_shapes=sum_scratch(width, points) + [
            pltpu.VMEM((sum(sizes), 2 * width), F32),
            pltpu.SMEM(rows.shape, rows.dtype),
            pltpu.SemaphoreType.DMA,
        ],
        compiler_params=params(),
        cost_estimate=cost(4.0),
        name="forward",
    )(rows, a, cs, q, other)


def more_rows(rows, q, lists, local):
    sizes = [len(owners) * local for owners in lists]

    def kernel(row_ref, q_ref, *refs):
        out_refs, stage_ref = refs[:-1], refs[-1]
        gather_rows(row_ref, q_ref, stage_ref, sum(lists, []), local)
        at = 0
        for ref in out_refs:
            ref[...] = stage_ref[at : at + ref.shape[0], :].astype(BF16)
            at += ref.shape[0]

    return pl.pallas_call(
        kernel,
        out_shape=tuple(jax.ShapeDtypeStruct((size, q.shape[1]), BF16) for size in sizes),
        in_specs=[smem()] + [vmem()],
        out_specs=(vmem(),) * len(sizes),
        scratch_shapes=[pltpu.VMEM((sum(sizes), q.shape[1]), F32)],
        compiler_params=params(),
        cost_estimate=cost(1.5),
        name="more_rows",
    )(rows, q)


def keep_rows(rows, q, owners, local):
    def kernel(row_ref, q_ref, out_ref):
        gather_rows(row_ref, q_ref, out_ref, owners, local)

    return pl.pallas_call(
        kernel,
        out_shape=jax.ShapeDtypeStruct((len(owners) * local, q.shape[1]), F32),
        in_specs=[smem()] + [vmem()],
        out_specs=vmem(),
        compiler_params=params(),
        cost_estimate=cost(2.0),
        name="keep_rows",
    )(rows, q)


def merge(keep, got, keep_at, got_at, rows):
    def kernel(keep_ref, got_ref, out_ref):
        total = keep_ref[keep_at : keep_at + rows, :]
        total = total + got_ref[got_at : got_at + rows, :].astype(F32)
        out_ref[...] = total.astype(BF16)

    return pl.pallas_call(
        kernel,
        out_shape=jax.ShapeDtypeStruct((rows, got.shape[1]), BF16),
        in_specs=[vmem()] * 2,
        out_specs=vmem(),
        compiler_params=params(),
        cost_estimate=cost(0.2),
        name="merge",
    )(keep, got)


def mix(keep, gots, flip, weights, layer, scale):
    modes, double = flip.shape[1], keep.shape[1]
    width = double // 2
    block = 16

    def kernel(flip_ref, w_ref, keep_ref, *refs):
        got_refs, (out_ref, s_ref, acc_ref) = refs[:-3], refs[-3:]
        total = keep_ref[:modes, :]
        for ref in got_refs:
            total = total + ref[:modes, :].astype(F32)
        s_ref[...] = total.T
        s_ref[width:, :] = s_ref[width:, :] * flip_ref[...]

        for at in range(0, width, block):

            def add(i, carry, at=at):
                real, imag = carry
                re = s_ref[pl.ds(i, 1), :]
                im = s_ref[pl.ds(width + i, 1), :]
                wr = w_ref[layer, 0, i, at : at + block].astype(F32)
                wi = w_ref[layer, 1, i, at : at + block].astype(F32)
                return real + re * wr - im * wi, imag + re * wi + im * wr

            zero = jnp.zeros((block, modes), F32)
            real, imag = lax.fori_loop(0, width, add, (zero, zero), unroll=16)
            acc_ref[at : at + block, :] = real * scale
            acc_ref[width + at : width + at + block, :] = imag * (flip_ref[...] * scale)

        out_ref[...] = acc_ref[...].T.astype(BF16)

    return pl.pallas_call(
        kernel,
        out_shape=jax.ShapeDtypeStruct((modes, double), BF16),
        in_specs=[vmem()] * (3 + len(gots)),
        out_specs=vmem(),
        scratch_shapes=[pltpu.VMEM((double, modes), F32), pltpu.VMEM((double, modes), F32)],
        compiler_params=params(),
        cost_estimate=cost(1.8),
        name="mix",
    )(flip, weights, keep, *gots)


def place_rows(place_ref, m_ref, z_ref, owners, local):
    me = lax.axis_index("pts")
    for at, owner in enumerate(owners):
        base = jnp.bitwise_xor(me, owner) * local

        def step(j, carry, base=base, at=at):
            z_ref[pl.ds(place_ref[base + j], 1), :] = m_ref[pl.ds(at * local + j, 1), :]
            return carry

        lax.fori_loop(0, local, step, 0, unroll=32)


def clear_table(double):
    def kernel(z_ref):
        def clear(i, carry):
            z_ref[pl.ds(pl.multiple_of(i * 32, 32), 32), :] = jnp.zeros((32, double), F32)
            return carry

        lax.fori_loop(0, 2 * ROWS_Q // 32, clear, 0, unroll=6)

    return pl.pallas_call(
        kernel,
        out_shape=jax.ShapeDtypeStruct((2 * ROWS_Q, double), F32),
        out_specs=vmem(),
        compiler_params=params(),
        cost_estimate=cost(0.8),
        name="clear_table",
    )()


def place_pieces(places, z, pieces, owners, local):
    double = pieces[0].shape[1]
    count = len(owners) * local
    n = len(pieces)

    def kernel(place_ref, before_ref, *refs):
        z_ref, m_ref = refs[n:]
        at = 0
        for ref in refs[:n]:
            m_ref[at : at + ref.shape[0], :] = ref[...].astype(F32)
            at += ref.shape[0]
        place_rows(place_ref, m_ref, z_ref, owners, local)

    return pl.pallas_call(
        kernel,
        out_shape=jax.ShapeDtypeStruct(z.shape, F32),
        in_specs=[smem()] + [vmem()] * (n + 1),
        out_specs=vmem(),
        input_output_aliases={1: 0},
        scratch_shapes=[pltpu.VMEM((count, double), F32)],
        compiler_params=params(),
        cost_estimate=cost(0.5 + 0.45 * count / 256),
        name="place_pieces",
    )(places, z, *pieces)


def evaluate(t_ref, a_ref, cs_ref, start, points, width, write):
    chunk = math.gcd(points, 512)
    for at in range(0, points, chunk):
        here = slice(start + at, start + at + chunk)
        r = lax.dot_general(
            t_ref[...], a_ref[:, here], (((1,), (0,)), ((), ())), preferred_element_type=F32
        )
        total = r[:width]
        for k in range(1, KZ):
            lo = 2 * k * width
            total = total + r[lo : lo + width] * cs_ref[k : k + 1, here]
            total = total + r[lo + width : lo + 2 * width] * cs_ref[16 + k : 17 + k, here]
        write(slice(at, at + chunk), total)


def inverse_other(places, z, piece, a, cs, owners, local):
    double = piece.shape[1]
    width = double // 2
    points = a.shape[1] // 2

    def kernel(list_ref, z_ref, piece_ref, a_ref, cs_ref, other_ref, t_ref, zz_ref, m_ref, place_ref, sem):
        copy = pltpu.make_async_copy(list_ref, place_ref, sem)
        copy.start()
        m_ref[...] = piece_ref[...].astype(F32)
        copy.wait()
        place_rows(place_ref, m_ref, zz_ref, owners, local)
        sign = sign_lanes(width)

        def combine(i, carry):
            base = pl.multiple_of(i * 32, 32)
            u, v = [], []
            for y in range(2):
                lo = base + 16 * y
                plus = zz_ref[pl.ds(lo, 8), :] + zz_ref[pl.ds(ROWS_Q + lo, 8), :]
                minus = zz_ref[pl.ds(lo + 8, 8), :] + zz_ref[pl.ds(ROWS_Q + lo + 8, 8), :]
                u.append(plus * sign + minus)
                v.append(pltpu.roll(plus - minus * sign, width, 1))
            zz_ref[pl.ds(base, 8), :] = u[0] + u[1]
            zz_ref[pl.ds(base + 8, 8), :] = v[1] - v[0]
            zz_ref[pl.ds(base + 16, 8), :] = -v[0] - v[1]
            zz_ref[pl.ds(base + 24, 8), :] = u[1] - u[0]
            return carry

        lax.fori_loop(0, KZ * GROUPS, combine, 0, unroll=9)
        for k in range(KZ):
            t_ref[k * double : (k + 1) * double, :] = zz_ref[
                k * ROWS_A : (k + 1) * ROWS_A, :
            ].T.astype(BF16)

        def write(here, total):
            other_ref[:, here] = total

        evaluate(t_ref, a_ref, cs_ref, points, points, width, write)

    return pl.pallas_call(
        kernel,
        out_shape=(
            jax.ShapeDtypeStruct((width, points), F32),
            jax.ShapeDtypeStruct((KZ * double, ROWS_A), BF16),
            jax.ShapeDtypeStruct(z.shape, F32),
        ),
        in_specs=[pl.BlockSpec(memory_space=pl.ANY)] + [vmem()] * 4,
        out_specs=(vmem(), vmem(), vmem()),
        input_output_aliases={1: 2},
        scratch_shapes=[
            pltpu.VMEM(piece.shape, F32),
            pltpu.SMEM(places.shape, places.dtype),
            pltpu.SemaphoreType.DMA,
        ],
        compiler_params=params(),
        cost_estimate=cost(4.5),
        name="inverse_other",
    )(places, z, piece, a, cs)[:2]


def inverse_own(t, a, cs, field, weight, bias, layer):
    width, points = field.shape

    def kernel(t_ref, a_ref, cs_ref, field_ref, weight_ref, bias_ref, out_ref):
        diagonal = lax.broadcasted_iota(jnp.int32, (width, width), 0) == lax.broadcasted_iota(
            jnp.int32, (width, width), 1
        )
        row = bias_ref[layer : layer + 1, :]
        column = jnp.sum(jnp.where(diagonal, row, 0.0), axis=1, keepdims=True)

        def write(here, total):
            direct = lax.dot_general(
                weight_ref[layer],
                field_ref[:, here],
                (((0,), (0,)), ((), ())),
                preferred_element_type=F32,
            )
            out_ref[:, here] = total + direct + column

        evaluate(t_ref, a_ref, cs_ref, 0, points, width, write)

    return pl.pallas_call(
        kernel,
        out_shape=jax.ShapeDtypeStruct((width, points), F32),
        in_specs=[vmem()] * 6,
        out_specs=vmem(),
        compiler_params=params(),
        cost_estimate=cost(2.1),
        name="inverse_own",
    )(t, a, cs, field, weight, bias)


def finish(own, got):
    def kernel(own_ref, got_ref, out_ref):
        x = own_ref[...] + got_ref[...]
        out_ref[...] = (0.5 * x * (1.0 + lax.erf(x * math.sqrt(0.5)))).astype(BF16)

    return pl.pallas_call(
        kernel,
        out_shape=jax.ShapeDtypeStruct(own.shape, BF16),
        in_specs=[vmem()] * 2,
        out_specs=vmem(),
        compiler_params=params(),
        cost_estimate=cost(0.8),
        name="finish",
    )(own, got)


def body(coords, field, mode_list, spec_weight, bypass_weight, bypass_bias):
    width, points = field.shape
    modes_total = mode_list.shape[0]
    count = lax.axis_size("pts")
    bits = count.bit_length() - 1
    me = lax.axis_index("pts")
    local = modes_total // count
    norm = 1.0 / math.sqrt(points * count)
    scale = 1.0 / math.sqrt(modes_total)

    def swap(x, mask):
        return lax.ppermute(x, "pts", [(i, i ^ mask) for i in range(count)])

    rows, flip = table_rows(mode_list)
    places = rows + jnp.where(flip, ROWS_Q, 0)
    signs = jnp.where(flip, -1.0, 1.0).astype(F32)
    my_signs = lax.dynamic_slice(signs, (me * local,), (local,)).reshape(1, local)
    owners = owners_of(count)
    near, far = owners[: count // 4], owners[count // 4 :]
    weights = jnp.transpose(spec_weight, (0, 2, 3, 4, 1))

    quarter = count // 16
    part = quarter * local
    near = [near[n * quarter : (n + 1) * quarter] for n in range(4)]
    far = [far[n * quarter : (n + 1) * quarter] for n in range(4)]

    theirs = swap(field, 1)
    a, cs = make_tables(coords, swap(coords, 1))
    for depth in range(LAYERS):
        if depth:
            theirs = swap(field, 1)
        q = forward_own(a, cs, field, norm)
        q, send_both = forward(rows, a, cs, q, theirs, norm, [far[3]], local)
        send_three, send_rest = more_rows(rows, q, [far[1], far[0] + far[2]], local)
        got_both, got_three, got_rest = (swap(x, 2) for x in (send_both, send_three, send_rest))
        keep = keep_rows(rows, q, near[0] + near[1] + near[2] + near[3], local)
        gots = [
            swap(merge(keep, got_both, 3 * part, 0, part), 12),
            swap(merge(keep, got_three, part, 0, part), 8),
            swap(merge(keep, got_rest, 2 * part, part, part), 4),
            got_rest,
        ]
        for bit in range(4, bits):
            total = keep[:part] if bit == 4 else keep
            for got in gots:
                total = total + got[: total.shape[0]].astype(F32)
            half = total.shape[0] // 2
            keep = total[:half]
            gots = [swap(total[half:].astype(BF16), 1 << bit)]
        pieces = mix(keep, gots, my_signs, weights, depth, scale)
        z = clear_table(2 * width)
        for bit in range(bits - 1, 3, -1):
            pieces = jnp.concatenate([pieces, swap(pieces, 1 << bit)], 0)
        over = [swap(pieces, mask) for mask in (8, 12, 4)]
        far_first = swap(pieces, 2)
        far_next = swap(jnp.concatenate(over[:2], 0), 2)
        last = swap(over[2], 2)
        z = place_pieces(places, z, [pieces], near[0], local)
        z = place_pieces(
            places, z, [far_first] + over, far[0] + near[1] + near[3] + near[2], local
        )
        z = place_pieces(places, z, [far_next], far[1] + far[3], local)
        theirs, t = inverse_other(places, z, last, a, cs, far[2], local)
        got = swap(theirs, 1)
        own = inverse_own(t, a, cs, field, bypass_weight, bypass_bias, depth)
        field = finish(own, got)
    return field


def solution(mesh):
    placed = (
        P(None, ("group", "pts")),
        P(None, ("group", "pts")),
        P(),
        P(None, "pts", None, None, None),
        P(),
        P(),
    )
    return jax.shard_map(
        body, mesh=mesh, in_specs=placed, out_specs=P(None, ("group", "pts")), check_vma=False
    )
```

```python
import math

import jax
import jax.numpy as jnp
from jax import lax
from jax.experimental import pallas as pl
from jax.experimental.pallas import tpu as pltpu
from jax.sharding import PartitionSpec as P

KDIM = 16
GRID = 1024
LAYERS = 2
TWO_PI = 2.0 * math.pi
HALF = KDIM // 2
KZ = HALF + 1
GROUPS = HALF + 3
ROWS_A = GROUPS * 32
ROWS_Q = KZ * ROWS_A
VMEM = 24 * 1024 * 1024
F32 = jnp.float32
BF16 = jnp.bfloat16


def cost(microseconds):
    return pl.CostEstimate(flops=int(microseconds * 1.1e9), bytes_accessed=0, transcendentals=0)


def params():
    return pltpu.CompilerParams(vmem_limit_bytes=VMEM)


def vmem():
    return pl.BlockSpec(memory_space=pltpu.VMEM)


def smem():
    return pl.BlockSpec(memory_space=pltpu.SMEM)


def table_rows(mode_list):
    kx = mode_list // (KDIM * KDIM) - HALF
    ky = mode_list // KDIM % KDIM - HALF
    kz = mode_list % KDIM - HALF
    flip = kx < 0
    ky = jnp.where(flip, -ky, ky)
    kz = jnp.where(flip, -kz, kz)
    ax, ay, az = jnp.abs(kx), jnp.abs(ky), jnp.abs(kz)
    quarter = 2 * (ky < 0).astype(jnp.int32) + (kz < 0).astype(jnp.int32)
    group = jnp.where(ay < HALF, ax, jnp.where(ax < HALF, HALF + 1, HALF + 2))
    inner = jnp.where(ay < HALF, ay, jnp.where(ax < HALF, ax, 0))
    row = ((az * GROUPS + group) * 4 + quarter) * 8 + inner
    return row, flip


def tables_kernel(own_ref, other_ref, a_ref, cs_ref):
    points = jnp.concatenate([own_ref[...], other_ref[...]], 1)
    angle = points.astype(F32) * (TWO_PI / GRID)
    one_c, one_s = jnp.cos(angle), jnp.sin(angle)
    cos, sin = [jnp.ones_like(angle), one_c], [jnp.zeros_like(angle), one_s]
    for k in range(2, HALF + 1):
        i, j = k // 2, k - k // 2
        cos.append(cos[i] * cos[j] - sin[i] * sin[j])
        sin.append(sin[i] * cos[j] + cos[i] * sin[j])
    cx = jnp.concatenate([c[0:1] for c in cos[:HALF]], 0)
    sx = jnp.concatenate([s[0:1] for s in sin[:HALF]], 0)
    cy = jnp.concatenate([c[1:2] for c in cos[:HALF]], 0)
    sy = jnp.concatenate([s[1:2] for s in sin[:HALF]], 0)
    for g in range(GROUPS):
        if g <= HALF:
            c, s = cos[g][0:1], sin[g][0:1]
            parts = [c * cy, c * sy, s * cy, s * sy]
        elif g == HALF + 1:
            c, s = cos[HALF][1:2], sin[HALF][1:2]
            parts = [cx * c, cx * s, sx * c, sx * s]
        else:
            c, s = cos[HALF][1:2], sin[HALF][1:2]
            first = (lax.broadcasted_iota(jnp.int32, cx.shape, 0) == 0).astype(F32)
            cl, sl = first * cos[HALF][0:1], first * sin[HALF][0:1]
            parts = [cl * c, cl * s, sl * c, sl * s]
        a_ref[g * 32 : (g + 1) * 32, :] = jnp.concatenate(parts, 0).astype(BF16)
    pad = jnp.zeros((7, angle.shape[1]), F32)
    cs_ref[...] = jnp.concatenate(
        [c[2:3] for c in cos] + [pad] + [s[2:3] for s in sin] + [pad], 0
    )


def make_tables(own, other):
    points = 2 * own.shape[1]
    return pl.pallas_call(
        tables_kernel,
        out_shape=(
            jax.ShapeDtypeStruct((ROWS_A, points), BF16),
            jax.ShapeDtypeStruct((32, points), F32),
        ),
        in_specs=[vmem()] * 2,
        out_specs=(vmem(), vmem()),
        compiler_params=params(),
        cost_estimate=cost(1.2),
        name="tables",
    )(own, other)


def sign_lanes(width):
    lane = lax.broadcasted_iota(jnp.int32, (8, 2 * width), 1)
    return jnp.where(lane < width, 1.0, -1.0).astype(F32)


def owners_of(count):
    bits = count.bit_length() - 1
    return [
        sum(((t >> (bits - 2 - b)) & 1) << (b + 1) for b in range(bits - 1))
        for t in range(count // 2)
    ]


def sums(norm, half, a_ref, cs_ref, h_ref, hs_ref, b_refs, write):
    width, points = h_ref.shape
    here = slice(half * points, (half + 1) * points)
    hs_ref[...] = h_ref[...].astype(F32) * norm

    def product(b):
        return lax.dot_general(
            a_ref[:, here], b, (((1,), (1,)), ((), ())), preferred_element_type=F32
        )

    first = product(hs_ref[...].astype(BF16))
    write(0, jnp.concatenate([first, jnp.zeros_like(first)], 1))
    for pair in range(HALF // 2):
        b_ref = b_refs[pair % 2]
        for part in range(2):
            k = 2 * pair + 1 + part
            b_ref[2 * part * width : (2 * part + 1) * width, :] = (
                hs_ref[...] * cs_ref[k : k + 1, here]
            ).astype(BF16)
            b_ref[(2 * part + 1) * width : (2 * part + 2) * width, :] = (
                hs_ref[...] * cs_ref[16 + k : 17 + k, here]
            ).astype(BF16)
        both = product(b_ref[...])
        write(2 * pair + 1, both[:, : 2 * width])
        write(2 * pair + 2, both[:, 2 * width :])


def combine_rows(q_ref, width):
    sign = sign_lanes(width)

    def combine(i, carry):
        base = pl.multiple_of(i * 32, 32)
        cc = q_ref[pl.ds(base, 8), :]
        cs = q_ref[pl.ds(base + 8, 8), :]
        sc = q_ref[pl.ds(base + 16, 8), :]
        ss = q_ref[pl.ds(base + 24, 8), :]
        for y in range(2):
            u = cc + ss if y else cc - ss
            v = pltpu.roll(sc - cs if y else sc + cs, width, 1)
            q_ref[pl.ds(base + 16 * y, 8), :] = u * sign - v
            q_ref[pl.ds(base + 16 * y + 8, 8), :] = u + v * sign
        return carry

    lax.fori_loop(0, KZ * GROUPS, combine, 0, unroll=9)


def sum_scratch(width, points):
    return [
        pltpu.VMEM((width, points), F32),
        pltpu.VMEM((4 * width, points), BF16),
        pltpu.VMEM((4 * width, points), BF16),
    ]


def forward_own(a, cs, own, norm):
    width, points = own.shape

    def kernel(a_ref, cs_ref, own_ref, q_ref, hs_ref, b0_ref, b1_ref):
        def write(k, total):
            q_ref[k * ROWS_A : (k + 1) * ROWS_A, :] = total

        sums(norm, 0, a_ref, cs_ref, own_ref, hs_ref, (b0_ref, b1_ref), write)

    return pl.pallas_call(
        kernel,
        out_shape=jax.ShapeDtypeStruct((ROWS_Q, 2 * width), F32),
        in_specs=[vmem()] * 3,
        out_specs=vmem(),
        scratch_shapes=sum_scratch(width, points),
        compiler_params=params(),
        cost_estimate=cost(2.0),
        name="forward_own",
    )(a, cs, own)


def gather_rows(row_ref, q_ref, out_ref, owners, local):
    me = lax.axis_index("pts")
    for at, owner in enumerate(owners):
        base = jnp.bitwise_xor(me, owner) * local

        def step(j, carry, base=base, at=at):
            out_ref[pl.ds(at * local + j, 1), :] = q_ref[pl.ds(row_ref[base + j], 1), :]
            return carry

        lax.fori_loop(0, local, step, 0, unroll=32)


def forward(rows, a, cs, q, other, norm, lists, local):
    width, points = other.shape
    sizes = [len(owners) * local for owners in lists]

    def kernel(list_ref, a_ref, cs_ref, before_ref, other_ref, q_ref, *refs):
        send_refs, (hs_ref, b0_ref, b1_ref, stage_ref, row_ref, sem) = refs[:-6], refs[-6:]
        copy = pltpu.make_async_copy(list_ref, row_ref, sem)
        copy.start()

        def write(k, total):
            here = slice(k * ROWS_A, (k + 1) * ROWS_A)
            q_ref[here, :] = before_ref[here, :] + total

        sums(norm, 1, a_ref, cs_ref, other_ref, hs_ref, (b0_ref, b1_ref), write)
        combine_rows(q_ref, width)
        copy.wait()
        gather_rows(row_ref, q_ref, stage_ref, sum(lists, []), local)
        at = 0
        for ref in send_refs:
            ref[...] = stage_ref[at : at + ref.shape[0], :].astype(BF16)
            at += ref.shape[0]

    return pl.pallas_call(
        kernel,
        out_shape=(jax.ShapeDtypeStruct((ROWS_Q, 2 * width), F32),)
        + tuple(jax.ShapeDtypeStruct((size, 2 * width), BF16) for size in sizes),
        in_specs=[pl.BlockSpec(memory_space=pl.ANY)] + [vmem()] * 4,
        out_specs=(vmem(),) * (1 + len(sizes)),
        scratch_shapes=sum_scratch(width, points) + [
            pltpu.VMEM((sum(sizes), 2 * width), F32),
            pltpu.SMEM(rows.shape, rows.dtype),
            pltpu.SemaphoreType.DMA,
        ],
        compiler_params=params(),
        cost_estimate=cost(4.0),
        name="forward",
    )(rows, a, cs, q, other)


def more_rows(rows, q, lists, local):
    sizes = [len(owners) * local for owners in lists]

    def kernel(row_ref, q_ref, *refs):
        out_refs, stage_ref = refs[:-1], refs[-1]
        gather_rows(row_ref, q_ref, stage_ref, sum(lists, []), local)
        at = 0
        for ref in out_refs:
            ref[...] = stage_ref[at : at + ref.shape[0], :].astype(BF16)
            at += ref.shape[0]

    return pl.pallas_call(
        kernel,
        out_shape=tuple(jax.ShapeDtypeStruct((size, q.shape[1]), BF16) for size in sizes),
        in_specs=[smem()] + [vmem()],
        out_specs=(vmem(),) * len(sizes),
        scratch_shapes=[pltpu.VMEM((sum(sizes), q.shape[1]), F32)],
        compiler_params=params(),
        cost_estimate=cost(1.5),
        name="more_rows",
    )(rows, q)


def keep_rows(rows, q, owners, local):
    def kernel(row_ref, q_ref, out_ref):
        gather_rows(row_ref, q_ref, out_ref, owners, local)

    return pl.pallas_call(
        kernel,
        out_shape=jax.ShapeDtypeStruct((len(owners) * local, q.shape[1]), F32),
        in_specs=[smem()] + [vmem()],
        out_specs=vmem(),
        compiler_params=params(),
        cost_estimate=cost(2.0),
        name="keep_rows",
    )(rows, q)


def merge(keep, got, keep_at, got_at, rows):
    def kernel(keep_ref, got_ref, out_ref):
        total = keep_ref[keep_at : keep_at + rows, :]
        total = total + got_ref[got_at : got_at + rows, :].astype(F32)
        out_ref[...] = total.astype(BF16)

    return pl.pallas_call(
        kernel,
        out_shape=jax.ShapeDtypeStruct((rows, got.shape[1]), BF16),
        in_specs=[vmem()] * 2,
        out_specs=vmem(),
        compiler_params=params(),
        cost_estimate=cost(0.2),
        name="merge",
    )(keep, got)


def mix(keep, gots, flip, weights, layer, scale):
    modes, double = flip.shape[1], keep.shape[1]
    width = double // 2
    block = 16

    def kernel(flip_ref, w_ref, keep_ref, *refs):
        got_refs, (out_ref, s_ref, acc_ref) = refs[:-3], refs[-3:]
        total = keep_ref[:modes, :]
        for ref in got_refs:
            total = total + ref[:modes, :].astype(F32)
        s_ref[...] = total.T
        s_ref[width:, :] = s_ref[width:, :] * flip_ref[...]

        for at in range(0, width, block):

            def add(i, carry, at=at):
                real, imag = carry
                re = s_ref[pl.ds(i, 1), :]
                im = s_ref[pl.ds(width + i, 1), :]
                wr = w_ref[layer, 0, i, at : at + block].astype(F32)
                wi = w_ref[layer, 1, i, at : at + block].astype(F32)
                return real + re * wr - im * wi, imag + re * wi + im * wr

            zero = jnp.zeros((block, modes), F32)
            real, imag = lax.fori_loop(0, width, add, (zero, zero), unroll=16)
            acc_ref[at : at + block, :] = real * scale
            acc_ref[width + at : width + at + block, :] = imag * (flip_ref[...] * scale)

        out_ref[...] = acc_ref[...].T.astype(BF16)

    return pl.pallas_call(
        kernel,
        out_shape=jax.ShapeDtypeStruct((modes, double), BF16),
        in_specs=[vmem()] * (3 + len(gots)),
        out_specs=vmem(),
        scratch_shapes=[pltpu.VMEM((double, modes), F32), pltpu.VMEM((double, modes), F32)],
        compiler_params=params(),
        cost_estimate=cost(1.8),
        name="mix",
    )(flip, weights, keep, *gots)


def place_rows(place_ref, m_ref, z_ref, owners, local):
    me = lax.axis_index("pts")
    for at, owner in enumerate(owners):
        base = jnp.bitwise_xor(me, owner) * local

        def step(j, carry, base=base, at=at):
            z_ref[pl.ds(place_ref[base + j], 1), :] = m_ref[pl.ds(at * local + j, 1), :]
            return carry

        lax.fori_loop(0, local, step, 0, unroll=32)


def clear_table(double):
    def kernel(z_ref):
        def clear(i, carry):
            z_ref[pl.ds(pl.multiple_of(i * 32, 32), 32), :] = jnp.zeros((32, double), F32)
            return carry

        lax.fori_loop(0, 2 * ROWS_Q // 32, clear, 0, unroll=6)

    return pl.pallas_call(
        kernel,
        out_shape=jax.ShapeDtypeStruct((2 * ROWS_Q, double), F32),
        out_specs=vmem(),
        compiler_params=params(),
        cost_estimate=cost(0.8),
        name="clear_table",
    )()


def place_pieces(places, z, pieces, owners, local):
    double = pieces[0].shape[1]
    count = len(owners) * local
    n = len(pieces)

    def kernel(place_ref, before_ref, *refs):
        z_ref, m_ref = refs[n:]
        at = 0
        for ref in refs[:n]:
            m_ref[at : at + ref.shape[0], :] = ref[...].astype(F32)
            at += ref.shape[0]
        place_rows(place_ref, m_ref, z_ref, owners, local)

    return pl.pallas_call(
        kernel,
        out_shape=jax.ShapeDtypeStruct(z.shape, F32),
        in_specs=[smem()] + [vmem()] * (n + 1),
        out_specs=vmem(),
        input_output_aliases={1: 0},
        scratch_shapes=[pltpu.VMEM((count, double), F32)],
        compiler_params=params(),
        cost_estimate=cost(0.5 + 0.45 * count / 256),
        name="place_pieces",
    )(places, z, *pieces)


def evaluate(t_ref, a_ref, cs_ref, start, points, width, write):
    chunk = math.gcd(points, 512)
    for at in range(0, points, chunk):
        here = slice(start + at, start + at + chunk)
        r = lax.dot_general(
            t_ref[...], a_ref[:, here], (((1,), (0,)), ((), ())), preferred_element_type=F32
        )
        total = r[:width]
        for k in range(1, KZ):
            lo = (2 * k - 1) * width
            total = total + r[lo : lo + width] * cs_ref[k : k + 1, here]
            total = total + r[lo + width : lo + 2 * width] * cs_ref[16 + k : 17 + k, here]
        write(slice(at, at + chunk), total)


def inverse_other(places, z, pieces, a, cs, owners, local):
    double = pieces[0].shape[1]
    n = len(pieces)
    width = double // 2
    points = a.shape[1] // 2

    def kernel(list_ref, z_ref, a_ref, cs_ref, *refs):
        other_ref, t_ref, zz_ref, m_ref, place_ref, sem = refs[n:]
        copy = pltpu.make_async_copy(list_ref, place_ref, sem)
        copy.start()
        at = 0
        for ref in refs[:n]:
            m_ref[at : at + ref.shape[0], :] = ref[...].astype(F32)
            at += ref.shape[0]
        copy.wait()
        place_rows(place_ref, m_ref, zz_ref, owners, local)
        sign = sign_lanes(width)

        def combine(i, carry):
            base = pl.multiple_of(i * 32, 32)
            u, v = [], []
            for y in range(2):
                lo = base + 16 * y
                plus = zz_ref[pl.ds(lo, 8), :] + zz_ref[pl.ds(ROWS_Q + lo, 8), :]
                minus = zz_ref[pl.ds(lo + 8, 8), :] + zz_ref[pl.ds(ROWS_Q + lo + 8, 8), :]
                u.append(plus * sign + minus)
                v.append(pltpu.roll(plus - minus * sign, width, 1))
            zz_ref[pl.ds(base, 8), :] = u[0] + u[1]
            zz_ref[pl.ds(base + 8, 8), :] = v[1] - v[0]
            zz_ref[pl.ds(base + 16, 8), :] = -v[0] - v[1]
            zz_ref[pl.ds(base + 24, 8), :] = u[1] - u[0]
            return carry

        lax.fori_loop(0, KZ * GROUPS, combine, 0, unroll=9)
        for k in range(KZ):
            block = zz_ref[k * ROWS_A : (k + 1) * ROWS_A, :].T.astype(BF16)
            if k == 0:
                t_ref[:width, :] = block[:width]
            else:
                t_ref[k * double - width : (k + 1) * double - width, :] = block

        def write(here, total):
            other_ref[:, here] = total

        evaluate(t_ref, a_ref, cs_ref, points, points, width, write)

    return pl.pallas_call(
        kernel,
        out_shape=(
            jax.ShapeDtypeStruct((width, points), F32),
            jax.ShapeDtypeStruct((KZ * double - width, ROWS_A), BF16),
            jax.ShapeDtypeStruct(z.shape, F32),
        ),
        in_specs=[pl.BlockSpec(memory_space=pl.ANY)] + [vmem()] * (3 + n),
        out_specs=(vmem(), vmem(), vmem()),
        input_output_aliases={1: 2},
        scratch_shapes=[
            pltpu.VMEM((len(owners) * local, double), F32),
            pltpu.SMEM(places.shape, places.dtype),
            pltpu.SemaphoreType.DMA,
        ],
        compiler_params=params(),
        cost_estimate=cost(4.5),
        name="inverse_other",
    )(places, z, a, cs, *pieces)[:2]


def inverse_own(t, a, cs, field, weight, bias, layer):
    width, points = field.shape

    def kernel(t_ref, a_ref, cs_ref, field_ref, weight_ref, bias_ref, out_ref):
        diagonal = lax.broadcasted_iota(jnp.int32, (width, width), 0) == lax.broadcasted_iota(
            jnp.int32, (width, width), 1
        )
        row = bias_ref[layer : layer + 1, :]
        column = jnp.sum(jnp.where(diagonal, row, 0.0), axis=1, keepdims=True)

        def write(here, total):
            direct = lax.dot_general(
                weight_ref[layer],
                field_ref[:, here],
                (((0,), (0,)), ((), ())),
                preferred_element_type=F32,
            )
            out_ref[:, here] = total + direct + column

        evaluate(t_ref, a_ref, cs_ref, 0, points, width, write)

    return pl.pallas_call(
        kernel,
        out_shape=jax.ShapeDtypeStruct((width, points), F32),
        in_specs=[vmem()] * 6,
        out_specs=vmem(),
        compiler_params=params(),
        cost_estimate=cost(2.1),
        name="inverse_own",
    )(t, a, cs, field, weight, bias)


def finish(own, got):
    def kernel(own_ref, got_ref, out_ref):
        x = own_ref[...] + got_ref[...]
        out_ref[...] = (0.5 * x * (1.0 + lax.erf(x * math.sqrt(0.5)))).astype(BF16)

    return pl.pallas_call(
        kernel,
        out_shape=jax.ShapeDtypeStruct(own.shape, BF16),
        in_specs=[vmem()] * 2,
        out_specs=vmem(),
        compiler_params=params(),
        cost_estimate=cost(0.8),
        name="finish",
    )(own, got)


def body(coords, field, mode_list, spec_weight, bypass_weight, bypass_bias):
    width, points = field.shape
    modes_total = mode_list.shape[0]
    count = lax.axis_size("pts")
    bits = count.bit_length() - 1
    me = lax.axis_index("pts")
    local = modes_total // count
    norm = 1.0 / math.sqrt(points * count)
    scale = 1.0 / math.sqrt(modes_total)

    def swap(x, mask):
        return lax.ppermute(x, "pts", [(i, i ^ mask) for i in range(count)])

    rows, flip = table_rows(mode_list)
    places = rows + jnp.where(flip, ROWS_Q, 0)
    signs = jnp.where(flip, -1.0, 1.0).astype(F32)
    my_signs = lax.dynamic_slice(signs, (me * local,), (local,)).reshape(1, local)
    owners = owners_of(count)
    near, far = owners[: count // 4], owners[count // 4 :]
    weights = jnp.transpose(spec_weight, (0, 2, 3, 4, 1))

    quarter = count // 16
    part = quarter * local
    near = [near[n * quarter : (n + 1) * quarter] for n in range(4)]
    far = [far[n * quarter : (n + 1) * quarter] for n in range(4)]

    theirs = swap(field, 1)
    a, cs = make_tables(coords, swap(coords, 1))
    for depth in range(LAYERS):
        if depth:
            theirs = swap(field, 1)
        q = forward_own(a, cs, field, norm)
        q, send_both, send_three = forward(rows, a, cs, q, theirs, norm, [far[3], far[1]], local)
        (send_rest,) = more_rows(rows, q, [far[0] + far[2]], local)
        got_both, got_three, got_rest = (swap(x, 2) for x in (send_both, send_three, send_rest))
        keep = keep_rows(rows, q, near[0] + near[1] + near[2] + near[3], local)
        gots = [
            swap(merge(keep, got_both, 3 * part, 0, part), 12),
            swap(merge(keep, got_three, part, 0, part), 8),
            swap(merge(keep, got_rest, 2 * part, part, part), 4),
            got_rest,
        ]
        for bit in range(4, bits):
            total = keep[:part] if bit == 4 else keep
            for got in gots:
                total = total + got[: total.shape[0]].astype(F32)
            half = total.shape[0] // 2
            keep = total[:half]
            gots = [swap(total[half:].astype(BF16), 1 << bit)]
        pieces = mix(keep, gots, my_signs, weights, depth, scale)
        z = clear_table(2 * width)
        for bit in range(bits - 1, 3, -1):
            pieces = jnp.concatenate([pieces, swap(pieces, 1 << bit)], 0)
        over = [swap(pieces, mask) for mask in (4, 12, 8)]
        far_first = swap(pieces, 2)
        far_next = swap(jnp.concatenate(over[:2], 0), 2)
        last = swap(over[2], 2)
        z = place_pieces(places, z, [pieces], near[0], local)
        z = place_pieces(
            places, z, [far_first] + over, far[0] + near[2] + near[3] + near[1], local
        )
        theirs, t = inverse_other(
            places, z, [far_next, last], a, cs, far[2] + far[3] + far[1], local
        )
        got = swap(theirs, 1)
        own = inverse_own(t, a, cs, field, bypass_weight, bypass_bias, depth)
        field = finish(own, got)
    return field


def solution(mesh):
    placed = (
        P(None, ("group", "pts")),
        P(None, ("group", "pts")),
        P(),
        P(None, "pts", None, None, None),
        P(),
        P(),
    )
    return jax.shard_map(
        body, mesh=mesh, in_specs=placed, out_specs=P(None, ("group", "pts")), check_vma=False
    )
```
